128 devices in a mesh: ctx: 8 (over x, core), grp: 8 (over z, y_lo), tp: 2 (over y_hi).
Axes of the slice: x: 4, y: 4 (y_hi: 2, y_lo: 2; y = y_hi * 2 + y_lo), z: 4, core: 2. Of those that a mesh axis runs over, the one named last changes fastest.
Arguments:
- queries: bfloat16 [8, 2048, 2560], P('grp', 'ctx', 'tp'), may hold values from -6 to 6
- keys: bfloat16 [8, 2048, 512], P('grp', 'ctx', 'tp'), may hold values from -6 to 6
- values: bfloat16 [8, 2048, 512], P('grp', 'ctx', 'tp'), may hold values from -6 to 6
- prefix_keys: bfloat16 [8, 2048, 512], P('grp', 'ctx', 'tp'), may hold values from -6 to 6
- prefix_values: bfloat16 [8, 2048, 512], P('grp', 'ctx', 'tp'), may hold values from -6 to 6
- rollout_group: int32 [8], P('grp'), may hold values from 0 to 7
- roll_length: int32 [8], P('grp'), may hold values from 512 to 2048, as said below
- advantage: float32 [8], P('grp'), may hold values from -4 to 4
- upstream: bfloat16 [8, 2048, 5120], P('grp', 'ctx', 'tp'), may hold values from -6 to 6
- w_out: bfloat16 [2560, 5120], P('tp'), may hold values from -0.125 to 0.125
Outputs:
- attended: bfloat16 [8, 2048, 2560], P('grp', 'ctx', 'tp')
- mixed: bfloat16 [8, 2048, 5120], P('grp', 'ctx', 'tp')
- grad_queries: bfloat16 [8, 2048, 2560], P('grp', 'ctx', 'tp')
- grad_keys: bfloat16 [8, 2048, 512], P('grp', 'ctx', 'tp')
- grad_values: bfloat16 [8, 2048, 512], P('grp', 'ctx', 'tp')
- grad_prefix_keys: bfloat16 [8, 2048, 512], P('grp', 'ctx', 'tp')
- grad_prefix_values: bfloat16 [8, 2048, 512], P('grp', 'ctx', 'tp')
The draws below stay inside these ranges and needn't reach their ends.
Inputs may be any that keep to these rules, and one draw needn't show every extreme that they name: `roll_length`: one rollout has the full length 2048.
All inputs are finite; a program needn't handle non-finite values.
Results may differ from the reference program's by a relative error of at most 0.03.
Values may be sent and summed in bfloat16 or wider, within the bound.
No kernel may reach another device: no remote copies, remote signals or barrier semaphores. Data moves between devices by JAX's collectives and lax.ppermute only.
A program may use at most 128 MiB of HBM per device.

```python
import jax
import jax.numpy as jnp
from jax import lax

D = 5120
QH = 20
KVH = 4
HD = 128
GROUPS = 8
ROLLOUTS = 8
ROLL_LEN = 2048
PREFIX_LEN = 2048


def draw_roll_length(key, part):
    key = jax.random.fold_in(key, 7)
    first, second = jax.random.split(key)
    lengths = jax.random.randint(first, (ROLLOUTS,), ROLL_LEN // 4, ROLL_LEN + 1)
    longest = jax.random.randint(second, (), 0, ROLLOUTS)
    return jnp.where(jnp.arange(ROLLOUTS) == longest, ROLL_LEN, lengths).astype(jnp.int32)


def with_ends(result, own_key, smallest, largest):
    spot = [jax.random.randint(jax.random.fold_in(own_key, axis), (), 0, length) for axis, length in enumerate(result.shape)]
    widest = result.shape.index(max(result.shape))
    next_to = spot[:widest] + [(spot[widest] + 1) % result.shape[widest]] + spot[widest + 1:]
    return result.at[tuple(spot)].set(smallest).at[tuple(next_to)].set(largest)


def shard_levels(stream_key, extent, pieces, low, high):
    loudness = 1.0
    for position, shards_of in pieces:
        draws = jax.random.uniform(jax.random.fold_in(jax.random.fold_in(stream_key, 6), position), (shards_of,), jnp.float32, low / len(pieces), high / len(pieces))
        loudness = loudness * jnp.repeat(jnp.exp(draws), extent[position] // shards_of).reshape((-1,) + (1,) * (len(extent) - 1 - position))
    return loudness


def gaussian(stream_key, dims, width, limit, shards=(), kind=jnp.bfloat16):
    entries = jax.random.normal(stream_key, dims, jnp.float32) * width
    if len(shards) > 0:
        entries = shard_levels(stream_key, dims, shards, -0.22, 0.18) * entries
    return jnp.clip(entries, min=-limit, max=limit).astype(kind)


def setup_inputs(seed: int = 0) -> dict:
    key_of = jax.random.split(jax.random.key(seed), 11)
    return {
        "queries": gaussian(key_of[0], (ROLLOUTS, ROLL_LEN, QH * HD), 1.0, 6.0, ((0, 8), (1, 8), (2, 2))),
        "keys": gaussian(key_of[1], (ROLLOUTS, ROLL_LEN, KVH * HD), 1.0, 6.0, ((0, 8), (1, 8), (2, 2))),
        "values": gaussian(key_of[2], (ROLLOUTS, ROLL_LEN, KVH * HD), 1.0, 6.0, ((0, 8), (1, 8), (2, 2))),
        "prefix_keys": gaussian(key_of[3], (GROUPS, PREFIX_LEN, KVH * HD), 1.0, 6.0, ((0, 8), (1, 8), (2, 2))),
        "prefix_values": gaussian(key_of[4], (GROUPS, PREFIX_LEN, KVH * HD), 1.0, 6.0, ((0, 8), (1, 8), (2, 2))),
        "rollout_group": with_ends(jax.random.randint(key_of[5], (ROLLOUTS,), 0, GROUPS), jax.random.fold_in(key_of[5], 1), 0, GROUPS - 1).astype(jnp.int32),
        "roll_length": draw_roll_length(jax.random.fold_in(key_of[10], 71), 0),
        "advantage": gaussian(key_of[7], (ROLLOUTS,), 1.0, 4.0, ((0, 8),), jnp.float32),
        "upstream": gaussian(key_of[8], (ROLLOUTS, ROLL_LEN, D), 1.0, 6.0, ((0, 8), (1, 8), (2, 2))),
        "w_out": gaussian(key_of[9], (QH * HD, D), (QH * HD) ** -0.5, 0.125, ((0, 2),)),
    }


big_negative = -1.0e30


def reference(queries, keys, values, prefix_keys, prefix_values, rollout_group, roll_length, advantage, upstream, w_out):
    share = QH // KVH
    scale = HD ** -0.5
    positions = jnp.arange(ROLL_LEN, dtype=jnp.int32)

    def one_rollout(carry, item):
        grad_pk, grad_pv = carry
        rows_q, row_k, row_v, group, length, adv, upper = item
        group = group.astype(jnp.int32)
        pre_k = lax.dynamic_index_in_dim(prefix_keys, group, 0, keepdims=False)
        pre_v = lax.dynamic_index_in_dim(prefix_values, group, 0, keepdims=False)
        all_k = jnp.concatenate([pre_k, row_k], axis=0).reshape(-1, KVH, HD).astype(jnp.float32)
        all_v = jnp.concatenate([pre_v, row_v], axis=0).reshape(-1, KVH, HD).astype(jnp.float32)
        q_four = rows_q.reshape(ROLL_LEN, KVH, share, HD).astype(jnp.float32)
        causal = (positions[None, :] <= positions[:, None]) & (positions[None, :] < length)
        allowed = jnp.concatenate([jnp.ones((ROLL_LEN, PREFIX_LEN), dtype=bool), causal], axis=1)[:, None, None, :]
        scores = jnp.einsum("tegd,sed->tegs", q_four, all_k) * scale
        scores = jnp.where(allowed, scores, big_negative)
        top = jnp.max(scores, axis=-1)
        lse = top + jnp.log(jnp.sum(jnp.where(allowed, jnp.exp(scores - top[..., None]), 0.0), axis=-1))
        probs = jnp.where(allowed, jnp.exp(scores - lse[..., None]), 0.0)
        probs_low = probs.astype(jnp.bfloat16).astype(jnp.float32)
        live = (positions < length).astype(jnp.float32)
        attended = (jnp.einsum("tegs,sed->tegd", probs_low, all_v) * live[:, None, None, None]).astype(jnp.bfloat16)
        flat = attended.reshape(ROLL_LEN, QH * HD)
        mixed = jnp.dot(flat, w_out, preferred_element_type=jnp.float32).astype(jnp.bfloat16)
        back = jnp.dot(upper, w_out.T, preferred_element_type=jnp.float32)
        grads = (back * (adv * live)[:, None]).astype(jnp.bfloat16).reshape(ROLL_LEN, KVH, share, HD).astype(jnp.float32)
        delta = jnp.sum(grads * attended.astype(jnp.float32), axis=-1)
        dprobs = jnp.einsum("tegd,sed->tegs", grads, all_v)
        dscores = (probs * (dprobs - delta[..., None])).astype(jnp.bfloat16).astype(jnp.float32)
        grad_q = (jnp.einsum("tegs,sed->tegd", dscores, all_k) * scale).astype(jnp.bfloat16)
        key_part = jnp.einsum("tegs,tegd->sed", dscores, q_four) * scale
        value_part = jnp.einsum("tegs,tegd->sed", probs_low, grads)
        key_flat = key_part.reshape(PREFIX_LEN + ROLL_LEN, KVH * HD)
        value_flat = value_part.reshape(PREFIX_LEN + ROLL_LEN, KVH * HD)
        old_k = lax.dynamic_index_in_dim(grad_pk, group, 0, keepdims=False)
        old_v = lax.dynamic_index_in_dim(grad_pv, group, 0, keepdims=False)
        grad_pk = lax.dynamic_update_index_in_dim(grad_pk, old_k + key_flat[:PREFIX_LEN], group, 0)
        grad_pv = lax.dynamic_update_index_in_dim(grad_pv, old_v + value_flat[:PREFIX_LEN], group, 0)
        results = (flat, mixed, grad_q.reshape(ROLL_LEN, QH * HD), key_flat[PREFIX_LEN:].astype(jnp.bfloat16), value_flat[PREFIX_LEN:].astype(jnp.bfloat16))
        return (grad_pk, grad_pv), results

    empty = jnp.zeros((GROUPS, PREFIX_LEN, KVH * HD), jnp.float32)
    carry, outs = lax.scan(one_rollout, (empty, empty), (queries, keys, values, rollout_group, roll_length, advantage, upstream))
    attended, mixed, grad_queries, grad_keys, grad_values = outs
    return (attended, mixed, grad_queries, grad_keys, grad_values, carry[0].astype(jnp.bfloat16), carry[1].astype(jnp.bfloat16))
```

```python
import functools
import jax
import jax.numpy as jnp
from jax import lax
from jax.experimental import pallas as pl
from jax.experimental.pallas import tpu as pltpu
from jax.sharding import PartitionSpec as P

HD = 128
TOK = 256
NQ = 10
NE = 2
SH = 5
LOG2E = 1.4426950408889634
SCALE = HD ** (-0.5)
SC2 = SCALE * LOG2E
NEG = -1e30
VMEM_LIMIT = 56 * 1024 * 1024


def _dot(a, b):
    return jnp.dot(a, b, preferred_element_type=jnp.float32)


def _load_all(shards, kv, sems):
    copies = [
        pltpu.make_async_copy(s, kv.at[:, pl.ds(i * TOK, TOK), :], sems.at[i])
        for i, s in enumerate(shards)
    ]
    for c in copies:
        c.start()
    return copies


def _fwd_chunk(kv, start, ck, q_ref, m_ref, l_ref, o_ref, mask=None):
    for e in range(NE):
        cols = slice(e * HD, (e + 1) * HD)
        k = kv[0, pl.ds(start, ck), cols]
        vt = kv[1, pl.ds(start, ck), cols].T
        for g in range(SH):
            h = e * SH + g
            s = _dot(k, q_ref[h])
            if mask is not None:
                s = jnp.where(mask, s, NEG)
            m_prev = m_ref[h]
            m_new = jnp.maximum(m_prev, jnp.max(s, axis=0, keepdims=True))
            p = jnp.exp2((s - m_new) * SC2)
            alpha = jnp.exp2((m_prev - m_new) * SC2)
            m_ref[h] = m_new
            l_ref[h] = l_ref[h] * alpha + jnp.sum(p, axis=0, keepdims=True)
            o_ref[h] = o_ref[h] * alpha + _dot(vt, p.astype(jnp.bfloat16))


def fwd_local_kernel(x_ref, q_ref, *refs):
    shards, (m_ref, l_ref, o_ref), (kv, sems) = refs[:8], refs[8:11], refs[11:]
    x, core = x_ref[0], x_ref[1]
    copies = _load_all(shards, kv, sems)
    m_ref[...] = jnp.full(m_ref.shape, NEG, jnp.float32)
    l_ref[...] = jnp.zeros(l_ref.shape, jnp.float32)
    o_ref[...] = jnp.zeros(o_ref.shape, jnp.float32)
    for c in copies:
        c.wait()
    mask = lax.broadcasted_iota(jnp.int32, (TOK, TOK), 0) <= lax.broadcasted_iota(
        jnp.int32, (TOK, TOK), 1
    )
    _fwd_chunk(kv, 0, TOK, q_ref, m_ref, l_ref, o_ref, mask)

    @pl.when(core == 1)
    def _():
        _fwd_chunk(kv, TOK, TOK, q_ref, m_ref, l_ref, o_ref)

    def body(d, _):
        _fwd_chunk(kv, pl.multiple_of(d * 2 * TOK, 2 * TOK), 2 * TOK, q_ref, m_ref, l_ref, o_ref)
        return 0

    lax.fori_loop(1, x + 1, body, 0)


def fwd_prefix_kernel(live_ref, q_ref, m0, l0, o0, *refs, ck):
    shards, (ot_ref, att_ref, lse_ref), (kv, m_ref, l_ref, o_ref, sems) = (
        refs[:8],
        refs[8:11],
        refs[11:],
    )
    copies = _load_all(shards, kv, sems)
    m_ref[...] = m0[...]
    l_ref[...] = l0[...]
    o_ref[...] = o0[...]
    for c in copies:
        c.wait()

    def body(d, _):
        _fwd_chunk(kv, pl.multiple_of(d * ck, ck), ck, q_ref, m_ref, l_ref, o_ref)
        return 0

    lax.fori_loop(0, 8 * TOK // ck, body, 0)
    live = live_ref[...]
    for h in range(NQ):
        total = l_ref[h]
        out = o_ref[h] * (live / total)
        ot_ref[h] = out.astype(jnp.bfloat16)
        att_ref[:, h * HD : (h + 1) * HD] = out.T.astype(jnp.bfloat16)
        lse_ref[h] = m_ref[h] * SC2 + jnp.log2(total)


def _bwd_chunk(kv, start, ck, q_ref, qn_ref, g_ref, gn_ref, lse_ref, dl, dq, ps, ds, store, mask=None):
    for e in range(NE):
        cols = slice(e * HD, (e + 1) * HD)
        k = kv[0, pl.ds(start, ck), cols]
        v = kv[1, pl.ds(start, ck), cols]
        kt = k.T
        for g in range(SH):
            h = e * SH + g
            s = _dot(k, q_ref[h])
            p = jnp.exp2(s * SC2 - lse_ref[h])
            if mask is not None:
                p = jnp.where(mask, p, 0.0)
            dp = _dot(v, g_ref[h])
            d = (p * (dp - dl[h])).astype(jnp.bfloat16)
            ps[:ck, g * TOK : (g + 1) * TOK] = p.astype(jnp.bfloat16)
            ds[:ck, g * TOK : (g + 1) * TOK] = d
            dq[h] += _dot(kt, d)
        store(
            e,
            (_dot(ds[:ck], qn_ref[e]) * SCALE).astype(jnp.bfloat16),
            _dot(ps[:ck], gn_ref[e]).astype(jnp.bfloat16),
        )


def _bwd_setup(g_ref, ot_ref, dl, dq):
    for h in range(NQ):
        dl[h] = jnp.sum(
            g_ref[h].astype(jnp.float32) * ot_ref[h].astype(jnp.float32), axis=0, keepdims=True
        )


def _store_to(outs, chip, side, ck):
    def store(e, dk, dv):
        cols = slice(e * HD, (e + 1) * HD)
        for i in range(ck // TOK):
            rows = slice(i * TOK, (i + 1) * TOK)
            out = outs[(side + i) % 2]
            out[chip + i // 2, 0, :, cols] = dk[rows]
            out[chip + i // 2, 1, :, cols] = dv[rows]

    return store


def bwd_prefix_kernel(q_ref, qn_ref, g_ref, gn_ref, ot_ref, lse_ref, *refs, ck):
    shards, (dq_ref, *outs), (kv, dl, ps, ds, sems) = refs[:8], refs[8:11], refs[11:]
    copies = _load_all(shards, kv, sems)
    _bwd_setup(g_ref, ot_ref, dl, dq_ref)
    dq_ref[...] = jnp.zeros(dq_ref.shape, jnp.float32)
    for c in copies:
        c.wait()

    def body(i, _):
        start = pl.multiple_of(i * ck, ck)
        _bwd_chunk(
            kv, start, ck, q_ref, qn_ref, g_ref, gn_ref, lse_ref, dl, dq_ref, ps, ds,
            _store_to(outs, i * (ck // (2 * TOK)), 0, ck),
        )
        return 0

    lax.fori_loop(0, 8 * TOK // ck, body, 0)


def bwd_local_kernel(x_ref, q_ref, qn_ref, g_ref, gn_ref, ot_ref, lse_ref, dq0_ref, *refs):
    shards, (dqo_ref, *outs), (kv, dl, dq, ps, ds, sems) = refs[:8], refs[8:11], refs[11:]
    x, core = x_ref[0], x_ref[1]
    copies = _load_all(shards, kv, sems)
    _bwd_setup(g_ref, ot_ref, dl, dq)
    dq[...] = dq0_ref[...]
    for c in copies:
        c.wait()
    mask = lax.broadcasted_iota(jnp.int32, (TOK, TOK), 0) <= lax.broadcasted_iota(
        jnp.int32, (TOK, TOK), 1
    )

    def run(chip, side, ck, m=None):
        start = pl.multiple_of(chip * 2 * TOK + side * TOK, TOK)
        _bwd_chunk(
            kv, start, ck, q_ref, qn_ref, g_ref, gn_ref, lse_ref, dl, dq, ps, ds,
            _store_to(outs, chip, side, ck), m,
        )

    run(0, 0, TOK, mask)

    @pl.when(core == 1)
    def _():
        run(0, 1, TOK)

    @pl.when(core == 0)
    def _():
        outs[1][0] = jnp.zeros((2, TOK, NE * HD), jnp.bfloat16)

    def body(d, _):
        run(d, 0, 2 * TOK)
        return 0

    lax.fori_loop(1, x + 1, body, 0)

    def blank(d, _):
        for out in outs:
            out[d] = jnp.zeros((2, TOK, NE * HD), jnp.bfloat16)
        return 0

    lax.fori_loop(x + 1, 4, blank, 0)
    for h in range(NQ):
        dqo_ref[:, h * HD : (h + 1) * HD] = (dq[h] * SCALE).T.astype(jnp.bfloat16)


VM = pl.BlockSpec(memory_space=pltpu.VMEM)
SM = pl.BlockSpec(memory_space=pltpu.SMEM)
HB = pl.BlockSpec(memory_space=pl.ANY)
F32 = jnp.float32
BF = jnp.bfloat16


def S(shape, dt):
    return jax.ShapeDtypeStruct(shape, dt)


def _cost(mults, el):
    return pl.CostEstimate(flops=2 * mults, bytes_accessed=4_000_000, transcendentals=el)


def _params():
    return pltpu.CompilerParams(vmem_limit_bytes=VMEM_LIMIT)


KV_S = pltpu.VMEM((2, 8 * TOK, NE * HD), BF)
ROW = (NQ, 1, TOK)
MAT = (NQ, HD, TOK)
PART = (4, 2, TOK, NE * HD)


def _el(keys):
    return NQ * TOK * keys


def fwd_local(xc, qt, shards):
    return pl.pallas_call(
        fwd_local_kernel,
        out_shape=(S(ROW, F32), S(ROW, F32), S(MAT, F32)),
        in_specs=[SM, VM] + [HB] * 8,
        out_specs=(VM, VM, VM),
        scratch_shapes=[KV_S, pltpu.SemaphoreType.DMA((8,))],
        compiler_params=_params(),
        cost_estimate=_cost(4 * _el(2048) * HD, _el(2048)),
        name="fwd_local",
    )(xc, qt, *shards)


def fwd_prefix(live, qt, state, shards, ck=2048):
    return pl.pallas_call(
        functools.partial(fwd_prefix_kernel, ck=ck),
        out_shape=(S(MAT, BF), S((TOK, NQ * HD), BF), S(ROW, F32)),
        in_specs=[VM] * 5 + [HB] * 8,
        out_specs=(VM, VM, VM),
        scratch_shapes=[
            KV_S,
            pltpu.VMEM(ROW, F32),
            pltpu.VMEM(ROW, F32),
            pltpu.VMEM(MAT, F32),
            pltpu.SemaphoreType.DMA((8,)),
        ],
        compiler_params=_params(),
        cost_estimate=_cost(4 * _el(2048) * HD, _el(2048)),
        name="fwd_prefix",
    )(live, qt, *state, *shards)


def bwd_prefix(qt, qn, gt, gn, ot, lse, shards, ck=1024):
    return pl.pallas_call(
        functools.partial(bwd_prefix_kernel, ck=ck),
        out_shape=(S(MAT, F32), S(PART, BF), S(PART, BF)),
        in_specs=[VM] * 6 + [HB] * 8,
        out_specs=(VM, VM, VM),
        scratch_shapes=[
            KV_S,
            pltpu.VMEM(ROW, F32),
            pltpu.VMEM((ck, SH * TOK), BF),
            pltpu.VMEM((ck, SH * TOK), BF),
            pltpu.SemaphoreType.DMA((8,)),
        ],
        compiler_params=_params(),
        cost_estimate=_cost(10 * _el(2048) * HD, _el(2048)),
        name="bwd_prefix",
    )(qt, qn, gt, gn, ot, lse, *shards)


def bwd_local(xc, qt, qn, gt, gn, ot, lse, dq0, shards):
    ck = 512
    return pl.pallas_call(
        bwd_local_kernel,
        out_shape=(S((TOK, NQ * HD), BF), S(PART, BF), S(PART, BF)),
        in_specs=[SM] + [VM] * 7 + [HB] * 8,
        out_specs=(VM, VM, VM),
        scratch_shapes=[
            KV_S,
            pltpu.VMEM(ROW, F32),
            pltpu.VMEM(MAT, F32),
            pltpu.VMEM((ck, SH * TOK), BF),
            pltpu.VMEM((ck, SH * TOK), BF),
            pltpu.SemaphoreType.DMA((8,)),
        ],
        compiler_params=_params(),
        cost_estimate=_cost(10 * _el(2048) * HD, _el(2048)),
        name="bwd_local",
    )(xc, qt, qn, gt, gn, ot, lse, dq0, *shards)


def back_kernel(col_ref, w_ref, up_ref, *refs):
    del col_ref
    acc = lax.dot_general(
        w_ref[...], up_ref[...], (((1,), (1,)), ((), ())), preferred_element_type=jnp.float32
    )
    if len(refs) == 1:
        refs[0][...] = acc
        return
    first_ref, row_ref, gt_ref, gn_ref = refs
    out = ((first_ref[...] + acc) * row_ref[...]).astype(jnp.bfloat16)
    gt_ref[...] = out
    gn_ref[0] = out.T


def back_part(col, w, up, first=None, row=None):
    half = up.shape[1]
    in_specs = [
        pl.BlockSpec((HD, half), lambda i, c: (i, c[0])),
        pl.BlockSpec((TOK, half), lambda i, c: (0, 0)),
    ]
    args = (w, up)
    if first is None:
        out_shape = S((NQ * HD, TOK), F32)
        out_specs = pl.BlockSpec((HD, TOK), lambda i, c: (i, 0))
    else:
        in_specs += [
            pl.BlockSpec((HD, TOK), lambda i, c: (i, 0)),
            pl.BlockSpec((1, TOK), lambda i, c: (0, 0)),
        ]
        args += (first, row)
        out_shape = (S((NQ * HD, TOK), BF), S((NQ, TOK, HD), BF))
        out_specs = (
            pl.BlockSpec((HD, TOK), lambda i, c: (i, 0)),
            pl.BlockSpec((1, TOK, HD), lambda i, c: (i, 0, 0)),
        )
    return pl.pallas_call(
        back_kernel,
        out_shape=out_shape,
        grid_spec=pltpu.PrefetchScalarGridSpec(
            num_scalar_prefetch=1, grid=(NQ,), in_specs=in_specs, out_specs=out_specs
        ),
        compiler_params=_params(),
        cost_estimate=pl.CostEstimate(
            flops=2 * NQ * HD * TOK * half, bytes_accessed=10_000_000, transcendentals=0
        ),
        name="back_part",
    )(col, *args)


def mix_kernel(col_ref, a_ref, w_ref, *refs):
    del col_ref
    acc = _dot(a_ref[...], w_ref[...])
    if len(refs) == 2:
        acc = acc + refs[0][...].astype(jnp.float32)
    refs[-1][...] = acc.astype(jnp.bfloat16)


def mix_part(col, att, w, other=None):
    half = w.shape[1] // 2
    width = 512
    steps = half // width
    in_specs = [
        pl.BlockSpec((TOK, NQ * HD), lambda i, c: (0, 0)),
        pl.BlockSpec((NQ * HD, width), lambda i, c: (0, c[0] * steps + i)),
    ]
    args = (att, w)
    out_spec = pl.BlockSpec((TOK, width), lambda i, c: (0, i))
    if other is not None:
        in_specs.append(out_spec)
        args += (other,)
    return pl.pallas_call(
        mix_kernel,
        out_shape=S((TOK, half), BF),
        grid_spec=pltpu.PrefetchScalarGridSpec(
            num_scalar_prefetch=1, grid=(steps,), in_specs=in_specs, out_specs=out_spec
        ),
        compiler_params=_params(),
        cost_estimate=pl.CostEstimate(
            flops=2 * NQ * HD * TOK * half, bytes_accessed=10_000_000, transcendentals=0
        ),
        name="mix_part",
    )(col, *args)


def xperm(dx, swap=0):
    return [(x * 2 + c, ((x + dx) % 4) * 2 + (c ^ swap)) for x in range(4) for c in range(2)]


SWAP = xperm(0, 1)


def ctx_gather(mine):
    same = [mine] + [lax.ppermute(mine, "ctx", xperm(d)) for d in (1, 2, 3)]
    out = []
    for s in same:
        out += [s, lax.ppermute(s, "ctx", SWAP)]
    return out


def ctx_reduce(same, other):
    got = lax.ppermute(other, "ctx", SWAP)
    parts = [same[d].astype(F32) + got[d].astype(F32) for d in range(4)]
    total = parts[0]
    for d in (1, 2, 3):
        total = total + lax.ppermute(parts[d].astype(BF), "ctx", xperm(-d)).astype(F32)
    return total


def pick(options, index):
    out = options[0]
    for i in range(1, len(options)):
        out = jnp.where(index == i, options[i], out)
    return out


def shards(
    queries,
    keys,
    values,
    prefix_keys,
    prefix_values,
    rollout_group,
    roll_length,
    advantage,
    upstream,
    w_out,
):
    ctx = lax.axis_index("ctx")
    grp = lax.axis_index("grp")
    tp = lax.axis_index("tp")
    x, core = ctx // 2, ctx % 2
    z, ylo = grp // 2, grp % 2
    xc = jnp.stack([x, core]).astype(jnp.int32)
    own_col = tp.reshape(1).astype(jnp.int32)
    other_col = (1 - tp).reshape(1).astype(jnp.int32)
    group = rollout_group[0]
    mate = lax.ppermute(rollout_group, "grp", SWAP)[0]
    positions = ctx * TOK + lax.iota(jnp.int32, TOK)
    live = (positions < roll_length[0]).astype(F32)[None]
    row = live * advantage[0]

    prefix = jnp.stack([prefix_keys[0], prefix_values[0]])
    local = jnp.stack([keys[0], values[0]])
    spread = [prefix] + [lax.ppermute(prefix, "grp", xperm(d)) for d in (1, 2, 3)]
    up_other = lax.ppermute(upstream[0], "tp", [(0, 1), (1, 0)])
    local_shards = ctx_gather(local)
    sent = pick(spread, (z - mate // 2) % 4)
    held = pick(spread, (z - group // 2) % 4)
    came = lax.ppermute(sent, "grp", SWAP)
    prefix_shards = ctx_gather(jnp.where(group % 2 == ylo, held, came))

    heads = queries[0].reshape(TOK, NQ, HD)
    qt = heads.transpose(1, 2, 0)
    qn = heads.transpose(1, 0, 2).reshape(NE, SH * TOK, HD)
    first = back_part(own_col, w_out, upstream[0])
    state = fwd_local(xc, qt, local_shards)
    gt, gn = back_part(other_col, w_out, up_other, first, row)
    gt = gt.reshape(MAT)
    gn = gn.reshape(NE, SH * TOK, HD)
    ot, att, lse = fwd_prefix(live, qt, state, prefix_shards)
    mix_other = lax.ppermute(mix_part(other_col, att, w_out), "tp", [(0, 1), (1, 0)])
    dq0, pre_same, pre_other = bwd_prefix(qt, qn, gt, gn, ot, lse, prefix_shards)
    column = ctx_reduce(pre_same, pre_other).astype(BF)
    theirs = lax.ppermute(column, "grp", SWAP)
    zero = jnp.zeros((), BF)

    def slot(target):
        a = jnp.where((group % 2 == ylo) & (group // 2 == target), column, zero)
        b = jnp.where((mate % 2 == ylo) & (mate // 2 == target), theirs, zero)
        return a.astype(F32) + b.astype(F32)

    owned = slot(z)
    for d in (1, 2, 3):
        owned = owned + lax.ppermute(
            slot((z + d) % 4).astype(BF), "grp", xperm(d)
        ).astype(F32)
    owned = owned.astype(BF)
    grad_queries, loc_same, loc_other = bwd_local(
        xc, qt, qn, gt, gn, ot, lse, dq0, local_shards
    )
    mixed = mix_part(own_col, att, w_out, mix_other)
    mine = ctx_reduce(loc_same, loc_other).astype(BF)
    return (
        att[None],
        mixed[None],
        grad_queries[None],
        mine[0][None],
        mine[1][None],
        owned[0][None],
        owned[1][None],
    )


def solution(mesh):
    spec = P("grp", "ctx", "tp")
    in_specs = (spec,) * 5 + (P("grp"),) * 3 + (spec, P("tp", None))
    return jax.shard_map(
        shards, mesh=mesh, in_specs=in_specs, out_specs=(spec,) * 7, check_vma=False
    )
```

```python
import functools

import jax
import jax.numpy as jnp
from jax import lax
from jax.experimental import pallas as pl
from jax.experimental.pallas import tpu as pltpu
from jax.sharding import PartitionSpec as P

HD = 128
TOK = 256
NQ = 10
NE = 2
SH = 5
SCALE = HD ** (-0.5)
SC2 = SCALE * 1.4426950408889634
NEG = -1e30
F32 = jnp.float32
BF = jnp.bfloat16
VM = pl.BlockSpec(memory_space=pltpu.VMEM)
SM = pl.BlockSpec(memory_space=pltpu.SMEM)
HB = pl.BlockSpec(memory_space=pl.ANY)
FAR = pl.BlockSpec(memory_space=pltpu.HBM)
ROW = (NQ, 1, TOK)
MAT = (NQ, HD, TOK)
EROW = (SH, 1, TOK)
EMAT = (SH, HD, TOK)


def S(shape, dt):
    return jax.ShapeDtypeStruct(shape, dt)


def call(kernel, name, outs, ins, scratch, args, keys, products, mib=16):
    mults = NQ * TOK * keys * HD * products
    return pl.pallas_call(
        kernel,
        out_shape=outs,
        in_specs=ins,
        out_specs=tuple(VM for _ in outs),
        scratch_shapes=scratch,
        compiler_params=pltpu.CompilerParams(vmem_limit_bytes=mib * 1024 * 1024),
        cost_estimate=pl.CostEstimate(
            flops=4 * mults, bytes_accessed=1_000_000, transcendentals=NQ * TOK * keys
        ),
        name=name,
    )(*args)


def dot(a, b):
    return jnp.dot(a, b, preferred_element_type=F32)


def pipeline(count, stages):
    held = [{} for _ in stages]
    for i in range(count + len(stages) - 1):
        for j, stage in enumerate(stages):
            t = i - j
            if 0 <= t < count:
                held[j][t] = stage(t, held[j - 1].pop(t) if j else None)


def start_loads(shards, kv, sems):
    copies = [
        pltpu.make_async_copy(s, kv.at[:, pl.ds(i * TOK, TOK), :], sems.at[i])
        for i, s in enumerate(shards)
    ]
    for c in copies:
        c.start()
    return copies


def causal():
    return lax.broadcasted_iota(jnp.int32, (TOK, TOK), 0) <= lax.broadcasted_iota(
        jnp.int32, (TOK, TOK), 1
    )


def forward(tasks, kv, q_ref, m_ref, l_ref, o_ref, mask=None):
    def scores(t, _):
        start, width, cols, hq, _h = tasks[t]
        s = dot(kv[0, pl.ds(start, width), cols], q_ref[hq])
        return s if mask is None else jnp.where(mask, s, NEG)

    def weigh(t, s):
        h = tasks[t][4]
        before = m_ref[h]
        top = jnp.maximum(before, jnp.max(s, axis=0, keepdims=True))
        p = jnp.exp2((s - top) * SC2)
        factor = jnp.exp2((before - top) * SC2)
        m_ref[h] = top
        l_ref[h] = l_ref[h] * factor + jnp.sum(p, axis=0, keepdims=True)
        return p.astype(BF), factor

    turned = {}

    def gather(t, item):
        start, width, cols, _hq, h = tasks[t]
        key = (t // SH, cols.start)
        if key not in turned:
            turned[key] = kv[1, pl.ds(start, width), cols].T
        o_ref[h] = o_ref[h] * item[1] + dot(turned[key], item[0])

    pipeline(len(tasks), [scores, weigh, gather])


def both_heads(start, width):
    return [
        (start, width, slice(e * HD, (e + 1) * HD), e * SH + g, e * SH + g)
        for e in range(NE)
        for g in range(SH)
    ]


def fwd_near_kernel(q_ref, mine, up_ref, *refs):
    m_ref, l_ref, o_ref, up_out, kv, sems, up_sem = refs[-7:]
    handed = pltpu.make_async_copy(up_ref, up_out, up_sem)
    handed.start()
    copies = start_loads((mine,), kv, sems)
    m_ref[...] = jnp.full(m_ref.shape, NEG, F32)
    l_ref[...] = jnp.zeros(l_ref.shape, F32)
    o_ref[...] = jnp.zeros(o_ref.shape, F32)
    copies[0].wait()
    forward(both_heads(0, TOK), kv, q_ref, m_ref, l_ref, o_ref, causal())
    handed.wait()


def fwd_far_kernel(x_ref, q_ref, m0, l0, o0, *refs, first, pairs):
    count = 2 * pairs + (1 if first else 0)
    shards, (m_ref, l_ref, o_ref, kv, sems) = refs[:count], refs[-5:]
    copies = start_loads(shards, kv, sems)
    m_ref[...] = m0[...]
    l_ref[...] = l0[...]
    o_ref[...] = o0[...]
    for c in copies:
        c.wait()

    def body(d, _):
        start = pl.multiple_of(d * 2 * TOK, 2 * TOK)
        forward(both_heads(start, 2 * TOK), kv, q_ref, m_ref, l_ref, o_ref)
        return 0

    lax.fori_loop(0, jnp.clip(x_ref[0] - first, 0, pairs), body, 0)
    if first:

        @pl.when(x_ref[1] == 1)
        def _():
            forward(both_heads(2 * pairs * TOK, TOK), kv, q_ref, m_ref, l_ref, o_ref)


def fwd_prefix_kernel(live_ref, q_ref, m0, l0, o0, *refs):
    shards, (ot_ref, att_ref, lse_ref, kv, m_ref, l_ref, o_ref, sems) = refs[:8], refs[-8:]
    copies = start_loads(shards, kv, sems)
    m_ref[...] = m0[...]
    l_ref[...] = l0[...]
    o_ref[...] = o0[...]
    for c in copies:
        c.wait()
    width = 4 * TOK

    def body(i, _):
        forward(both_heads(pl.multiple_of(i * width, width), width), kv, q_ref, m_ref, l_ref, o_ref)
        return 0

    lax.fori_loop(0, 2, body, 0)
    live = live_ref[...]
    for h in range(NQ):
        total = l_ref[h]
        out = o_ref[h] * (live / total)
        ot_ref[h] = out.astype(BF)
        att_ref[:, h * HD : (h + 1) * HD] = out.T.astype(BF)
        lse_ref[h] = m_ref[h] * SC2 + jnp.log2(total)


def backward(tasks, kv, q_ref, qn_ref, g_ref, gn_ref, lse_ref, dl, dq, ps, ds, store, mask=None):
    def products(t, _):
        start, width, cols, h, _s, _b = tasks[t]
        return (
            dot(kv[0, pl.ds(start, width), cols], q_ref[h]),
            dot(kv[1, pl.ds(start, width), cols], g_ref[h]),
        )

    def weigh(t, item):
        _start, width, _cols, h, s, b = tasks[t]
        p = jnp.exp2(item[0] * SC2 - lse_ref[h])
        if mask is not None:
            p = jnp.where(mask, p, 0.0)
        d = (p * (item[1] - dl[s])).astype(BF)
        g = h % SH
        ps[b, :width, g * TOK : (g + 1) * TOK] = p.astype(BF)
        ds[b, :width, g * TOK : (g + 1) * TOK] = d
        return d

    turned = {}

    def apply(t, d):
        start, width, cols, h, s, b = tasks[t]
        key = (t // SH, cols.start)
        if key not in turned:
            turned[key] = kv[0, pl.ds(start, width), cols].T
        dq[s] += dot(turned[key], d)
        if h % SH == SH - 1:
            e = h // SH
            queries = qn_ref[e * SH : (e + 1) * SH].reshape(SH * TOK, HD)
            grads = gn_ref[e * SH : (e + 1) * SH].reshape(SH * TOK, HD)
            store(
                t,
                (dot(ds[b, :width], queries) * SCALE).astype(BF),
                dot(ps[b, :width], grads).astype(BF),
            )

    pipeline(len(tasks), [products, weigh, apply])


def deltas(g_ref, ot_ref, dl):
    for h in range(NQ):
        dl[h] = jnp.sum(g_ref[h].astype(F32) * ot_ref[h].astype(F32), axis=0, keepdims=True)


def bwd_prefix_kernel(q_ref, qn_ref, g_ref, gn_ref, ot_ref, lse_ref, *refs):
    shards, (dq_ref, same, other, kv, dl, ps, ds, sems) = refs[:8], refs[-8:]
    copies = start_loads(shards, kv, sems)
    deltas(g_ref, ot_ref, dl)
    dq_ref[...] = jnp.zeros(dq_ref.shape, F32)
    for c in copies:
        c.wait()

    def body(d, _):
        local_backward(
            pl.multiple_of(d * 2 * TOK, 2 * TOK), 2 * TOK,
            (kv, q_ref, qn_ref, g_ref, gn_ref, lse_ref, dl, dq_ref, ps, ds),
            put_pair(same, other, d),
        )
        return 0

    lax.fori_loop(0, 4, body, 0)


def put_pair(same, other, d):
    def put(cols, dk, dv):
        for i, out in enumerate((same, other)):
            out[d, 0, :, cols] = dk[i * TOK : (i + 1) * TOK]
            out[d, 1, :, cols] = dv[i * TOK : (i + 1) * TOK]

    return put


def local_backward(start, width, refs, put, mask=None):
    kv, q_ref, qn_ref, g_ref, gn_ref, lse_ref, dl, dq, ps, ds = refs
    tasks = [
        (start, width, slice(e * HD, (e + 1) * HD), e * SH + g, e * SH + g, e)
        for e in range(NE)
        for g in range(SH)
    ]

    def store(t, dk, dv):
        e = t // SH
        put(slice(e * HD, (e + 1) * HD), dk, dv)

    backward(
        tasks, kv, q_ref, qn_ref, g_ref, gn_ref,
        lse_ref, dl, dq, ps, ds, store, mask,
    )


def bwd_far_kernel(x_ref, q_ref, qn_ref, g_ref, gn_ref, ot_ref, lse_ref, dq0, *refs):
    shards, (out_ref, same, other, kv, dl, dq_ref, ps, ds, sems) = refs[:6], refs[-9:]
    copies = start_loads(shards, kv, sems)
    deltas(g_ref, ot_ref, dl)
    dq_ref[...] = dq0[...]
    for c in copies:
        c.wait()

    def body(d, _):
        local_backward(
            pl.multiple_of(d * 2 * TOK, 2 * TOK), 2 * TOK,
            (kv, q_ref, qn_ref, g_ref, gn_ref, lse_ref, dl, dq_ref, ps, ds),
            put_pair(same, other, d),
        )
        return 0

    lax.fori_loop(0, x_ref[0], body, 0)

    def blank(d, _):
        same[d] = jnp.zeros(same.shape[1:], BF)
        other[d] = jnp.zeros(other.shape[1:], BF)
        return 0

    lax.fori_loop(x_ref[0], 3, blank, 0)
    for h in range(NQ):
        out_ref[:, h * HD : (h + 1) * HD] = (dq_ref[h] * SCALE).T.astype(BF)


def bwd_near_kernel(
    x_ref, q_ref, qn_ref, g_ref, gn_ref, ot_ref, lse_ref, dq0, mine, mate, *refs
):
    dq, same, other, kv, dl, ps, ds, sems = refs[-8:]
    copies = start_loads((mine, mate), kv, sems)
    deltas(g_ref, ot_ref, dl)
    dq[...] = dq0[...]
    for c in copies:
        c.wait()
    refs = (kv, q_ref, qn_ref, g_ref, gn_ref, lse_ref, dl, dq, ps, ds)

    def put_to(out):
        def put(cols, dk, dv):
            out[0, :, cols] = dk
            out[1, :, cols] = dv

        return put

    local_backward(0, TOK, refs, put_to(same), causal())

    @pl.when(x_ref[1] == 1)
    def _():
        local_backward(TOK, TOK, refs, put_to(other))

    @pl.when(x_ref[1] == 0)
    def _():
        other[...] = jnp.zeros(other.shape, BF)


def dma(*n):
    return pltpu.SemaphoreType.DMA(n)


def kv_scratch(keys, cols):
    return pltpu.VMEM((2, keys, cols), BF)


PAIR = (2, TOK, NE * HD)
HALF = (2, TOK, HD)


def fwd_near(qt, mine, up, *after):
    return call(
        fwd_near_kernel, "fwd_near",
        (S(ROW, F32), S(ROW, F32), S(MAT, F32), S(up.shape, BF)),
        [VM, HB, HB] + [HB] * len(after),
        [kv_scratch(TOK, NE * HD), dma(1), pltpu.SemaphoreType.DMA],
        (qt, mine, up, *after), 256, 2,
    )


def fwd_far(xc, qt, state, shards, first, *after):
    n = len(shards)
    return call(
        functools.partial(fwd_far_kernel, first=first, pairs=n // 2), "fwd_far",
        (S(ROW, F32), S(ROW, F32), S(MAT, F32)),
        [SM] + [VM] * 4 + [HB] * (n + len(after)),
        [kv_scratch(n * TOK, NE * HD), dma(n)], (xc, qt, *state, *shards, *after), 256 * n, 2,
    )


def fwd_prefix(live, qt, state, shards, *after):
    return call(
        fwd_prefix_kernel, "fwd_prefix", (S(MAT, BF), S((TOK, NQ * HD), BF), S(ROW, F32)),
        [VM] * 5 + [HB] * (8 + len(after)),
        [
            kv_scratch(8 * TOK, NE * HD), pltpu.VMEM(ROW, F32), pltpu.VMEM(ROW, F32),
            pltpu.VMEM(MAT, F32), dma(8),
        ],
        (live, qt, *state, *shards, *after), 2048, 2,
    )


def bwd_scratch(keys, width):
    return (
        [kv_scratch(keys, NE * HD), pltpu.VMEM(ROW, F32)]
        + [pltpu.VMEM((2, width, SH * TOK), BF)] * 2
        + [dma(keys // TOK)]
    )


def bwd_prefix(args, shards, *after):
    part = (4,) + PAIR
    return call(
        bwd_prefix_kernel, "bwd_prefix", (S(MAT, F32), S(part, BF), S(part, BF)),
        [VM] * 6 + [HB] * (8 + len(after)), bwd_scratch(8 * TOK, 2 * TOK),
        (*args, *shards, *after), 2048, 5,
    )


def bwd_far(xc, args, dq, shards, *after):
    part = (3,) + PAIR
    scratch = bwd_scratch(6 * TOK, 2 * TOK)
    return call(
        bwd_far_kernel, "bwd_far", (S((TOK, NQ * HD), BF), S(part, BF), S(part, BF)),
        [SM] + [VM] * 7 + [HB] * (6 + len(after)),
        scratch[:2] + [pltpu.VMEM(MAT, F32)] + scratch[2:],
        (xc, *args, dq, *shards, *after), 1536, 5,
    )


def bwd_near(xc, args, dq, mine, mate, *after):
    return call(
        bwd_near_kernel, "bwd_near", (S(MAT, F32), S(PAIR, BF), S(PAIR, BF)),
        [SM] + [VM] * 7 + [HB] * (2 + len(after)), bwd_scratch(2 * TOK, TOK),
        (xc, *args, dq, mine, mate, *after), 512, 5,
    )


def run_copies(pairs, sems):
    copies = [pltpu.make_async_copy(a, b, sems.at[i]) for i, (a, b) in enumerate(pairs)]
    for c in copies:
        c.start()
    return copies


def stack_kernel(k_ref, v_ref, out_ref, sems):
    for c in run_copies([(k_ref.at[0], out_ref.at[0]), (v_ref.at[0], out_ref.at[1])], sems):
        c.wait()


def stack_pair(k, v):
    return call(
        stack_kernel, "stack_pair", (S(PAIR, BF),), [FAR, FAR], [dma(2)], (k, v), 8, 1
    )[0]


def pick_kernel(index_ref, *refs):
    spread, outs, sems = refs[:4], refs[-3:-1], refs[-1]
    for o, out in enumerate(outs):
        for i, piece in enumerate(spread):

            @pl.when(index_ref[o] == i)
            def _():
                pltpu.make_async_copy(piece, out, sems.at[o]).start()

    for o, out in enumerate(outs):
        pltpu.make_async_copy(spread[0], out, sems.at[o]).wait()


def pick(indices, options, *after):
    return call(
        pick_kernel, "pick", (S(PAIR, BF),) * 2, [SM] + [HB] * (4 + len(after)), [dma(2)],
        (indices.astype(jnp.int32), *options, *after), 8, 1,
    )


def add_pairs_kernel(a_ref, b_ref, *refs, count):
    outs = refs[-count:]
    for d in range(count):
        outs[d][...] = (a_ref[d].astype(F32) + b_ref[d].astype(F32)).astype(BF)


def add_pairs(a, b, *after):
    n = a.shape[0]
    return call(
        functools.partial(add_pairs_kernel, count=n), "add_pairs", (S(PAIR, BF),) * n,
        [VM, VM] + [HB] * len(after), [], (a, b, *after), 8, 1,
    )


def add_all_kernel(*refs, count):
    total = refs[0][...].astype(F32)
    for ref in refs[1:count]:
        total = total + ref[...].astype(F32)
    refs[-1][...] = total.astype(BF)


def add_all(parts, *after):
    return call(
        functools.partial(add_all_kernel, count=len(parts)), "add_all", (S(PAIR, BF),),
        [VM] * len(parts) + [HB] * len(after), [], (*parts, *after), 8, 1,
    )[0]


def slot_kernel(flag_ref, a_ref, b_ref, *refs):
    a = a_ref[...].astype(F32)
    b = b_ref[...].astype(F32)
    for d, out in enumerate(refs[-4:]):
        out[...] = (
            jnp.where(flag_ref[d] == 1, a, 0.0) + jnp.where(flag_ref[4 + d] == 1, b, 0.0)
        ).astype(BF)


def slots(flags, a, b, *after):
    return call(
        slot_kernel, "slots", (S(PAIR, BF),) * 4, [SM, VM, VM] + [HB] * len(after), [],
        (flags, a, b, *after), 8, 1,
    )


def turn_kernel(q_ref, k_ref, v_ref, _first, *refs):
    qt_ref, qn_ref, pair_ref, q, sems = refs[-5:]
    copies = run_copies(
        [(q_ref.at[0], q), (k_ref.at[0], pair_ref.at[0]), (v_ref.at[0], pair_ref.at[1])], sems
    )
    copies[0].wait()
    for h in range(NQ):
        block = q[:, h * HD : (h + 1) * HD]
        qn_ref[h] = block
        qt_ref[h] = block.T
    copies[1].wait()
    copies[2].wait()


def turn(q, k, v, first):
    return call(
        turn_kernel, "turn", (S(MAT, BF), S((NQ, TOK, HD), BF), S(PAIR, BF)), [FAR] * 3 + [HB],
        [pltpu.VMEM((TOK, NQ * HD), BF), dma(3)], (q, k, v, first), 8, 1,
    )


def back_kernel(col_ref, w_ref, up_ref, *refs, last):
    w, sems = refs[-2:]
    half = up_ref.shape[1]
    rows = 2 * HD
    copies = []
    for i in range(NQ // 2):
        block = w_ref.at[pl.ds(i * rows, rows), pl.ds(pl.multiple_of(col_ref[0] * half, half), half)]
        copies.append(pltpu.make_async_copy(block, w.at[i], sems.at[i]))
        copies[-1].start()
    turned = up_ref[...].T
    for i, c in enumerate(copies):
        c.wait()
        acc = dot(w[i], turned)
        if not last:
            refs[-3][i * rows : (i + 1) * rows] = acc
            continue
        first_ref, row_ref = refs[:2]
        gt_ref, gn_ref = refs[-4:-2]
        out = ((first_ref[i * rows : (i + 1) * rows] + acc) * row_ref[...]).astype(BF)
        for j in range(2):
            gt_ref[2 * i + j] = out[j * HD : (j + 1) * HD]
            gn_ref[2 * i + j] = out[j * HD : (j + 1) * HD].T


def back_part(col, w, up, more=(), after=()):
    half = up.shape[1]
    outs = (S(MAT, BF), S((NQ, TOK, HD), BF)) if more else (S((NQ * HD, TOK), F32),)
    return call(
        functools.partial(back_kernel, last=bool(more)), "back_part", outs,
        [SM, FAR, VM] + [VM] * len(more) + [HB] * len(after),
        [pltpu.VMEM((NQ // 2, 2 * HD, half), BF), dma(NQ // 2)],
        (col, w, up, *more, *after), 1280, 1, 16 if more else 60,
    )


def mix_kernel(col_ref, a_ref, w_ref, *refs, last):
    out_ref, w, sems = refs[-3:]
    half = out_ref.shape[1]
    steps, _, width = w.shape
    copies = []
    for i in range(steps):
        first = pl.multiple_of(col_ref[0] * half + i * width, width)
        copies.append(pltpu.make_async_copy(w_ref.at[:, pl.ds(first, width)], w.at[i], sems.at[i]))
        copies[-1].start()
    a = a_ref[...]
    for i, c in enumerate(copies):
        c.wait()
        cols = slice(i * width, (i + 1) * width)
        acc = dot(a, w[i])
        if last:
            acc = acc + refs[0][:, cols].astype(F32)
        out_ref[:, cols] = acc.astype(BF)


def mix_part(col, att, w, more=(), after=()):
    half = w.shape[1] // 2
    width = 512
    return call(
        functools.partial(mix_kernel, last=bool(more)), "mix_part", (S((TOK, half), BF),),
        [SM, VM, FAR] + [VM] * len(more) + [HB] * len(after),
        [pltpu.VMEM((half // width, NQ * HD, width), BF), dma(half // width)],
        (col, att, w, *more, *after), 12800 if more else 1280, 1, 60 if more else 16,
    )[0]


def shift(d, swap=0):
    return [(x * 2 + c, ((x + d) % 4) * 2 + (c ^ swap)) for x in range(4) for c in range(2)]


SWAP = shift(0, 1)


def shards(
    queries, keys, values, prefix_keys, prefix_values, rollout_group, roll_length, advantage,
    upstream, w_out,
):
    ctx = lax.axis_index("ctx")
    grp = lax.axis_index("grp")
    tp = lax.axis_index("tp")
    x, core = ctx // 2, ctx % 2
    z, ylo = grp // 2, grp % 2
    xc = jnp.stack([x, core]).astype(jnp.int32)
    own_col = tp.reshape(1).astype(jnp.int32)
    other_col = 1 - own_col
    group = rollout_group[0]
    mate = lax.ppermute(rollout_group, "grp", SWAP)[0]
    positions = ctx * TOK + lax.iota(jnp.int32, TOK)
    live = (positions < roll_length[0]).astype(F32)[None]
    row = live * advantage[0]

    prefix = stack_pair(prefix_keys, prefix_values)
    spread = [prefix] + [lax.ppermute(prefix, "grp", shift(d)) for d in (1, 2, 3)]
    first = back_part(own_col, w_out, upstream[0])[0]
    qt, qn, local = turn(queries, keys, values, first)
    local_same = [local] + [lax.ppermute(local, "ctx", shift(d)) for d in (1, 2, 3)]
    local_mate = [lax.ppermute(s, "ctx", SWAP) for s in local_same]
    far = [s for d in (1, 2, 3) for s in (local_same[d], local_mate[d])]

    places = jnp.stack([(z - mate // 2) % 4, (z - group // 2) % 4])
    sent, held = pick(places, spread, qt)
    came = lax.ppermute(sent, "grp", SWAP)
    own = jnp.where(group % 2 == ylo, held, came)
    own_same = [own] + [lax.ppermute(own, "ctx", shift(d)) for d in (1, 2, 3)]
    *state, up = fwd_near(qt, local, upstream[0], own)
    up_other = lax.ppermute(up, "tp", [(0, 1), (1, 0)])
    state = fwd_far(xc, qt, state, far[:4], 0)
    mates = [
        lax.ppermute(own, "ctx", SWAP)
    ] + [lax.ppermute(s, "ctx", SWAP) for s in own_same[1:]]
    state = fwd_far(xc, qt, state, far[4:] + [local_mate[0]], 2, *own_same[1:])
    prefix_shards = [p for pair in zip(own_same, mates) for p in pair]
    ot, att, lse = fwd_prefix(live, qt, state, prefix_shards)
    half = mix_part(other_col, att, w_out)
    mix_other = lax.ppermute(half, "tp", [(0, 1), (1, 0)])
    gt, gn = back_part(other_col, w_out, up_other, (first, row), (half,))
    args = (qt, qn, gt, gn, ot, lse)

    dq, same, other = bwd_prefix(args, prefix_shards)
    got = lax.ppermute(other, "ctx", SWAP)
    dq, near_same, near_other = bwd_near(xc, args, dq, local, local_mate[0])
    sums = add_pairs(same, got, near_same)
    moved = [lax.ppermute(sums[d], "ctx", shift(-d)) for d in (1, 2, 3)]
    grad_queries, far_same, far_other = bwd_far(xc, args, dq, far, sums[0], mix_other)
    column = add_all([sums[0]] + moved, far_same)
    theirs = lax.ppermute(column, "grp", SWAP)
    mixed = mix_part(own_col, att, w_out, (mix_other,), (column,))
    far_sums = add_pairs(far_same, lax.ppermute(far_other, "ctx", SWAP), mixed)
    target = (z + lax.iota(jnp.int32, 4)) % 4
    flags = jnp.concatenate(
        [(g % 2 == ylo) & (g // 2 == target) for g in (group, mate)]
    ).astype(jnp.int32)
    placed = slots(flags, column, theirs, far_sums[0])
    arrived = [lax.ppermute(placed[d], "grp", shift(d)) for d in (1, 2, 3)]
    near = [near_same, lax.ppermute(near_other, "ctx", SWAP)]
    near += [lax.ppermute(far_sums[d - 1], "ctx", shift(-d)) for d in (1, 2, 3)]
    owned = add_all([placed[0]] + arrived)
    mine = add_all(near)
    return (
        att[None],
        mixed[None],
        grad_queries[None],
        mine[0][None],
        mine[1][None],
        owned[0][None],
        owned[1][None],
    )


def solution(mesh):
    spec = P("grp", "ctx", "tp")
    in_specs = (spec,) * 5 + (P("grp"),) * 3 + (spec, P("tp", None))
    return jax.shard_map(
        shards, mesh=mesh, in_specs=in_specs, out_specs=(spec,) * 7, check_vma=False
    )
```

```python
import functools

import jax
import jax.numpy as jnp
from jax import lax
from jax.experimental import pallas as pl
from jax.experimental.pallas import tpu as pltpu
from jax.sharding import PartitionSpec as P

HD = 128
TOK = 256
NQ = 10
NE = 2
SH = 5
SCALE = HD ** (-0.5)
SC2 = SCALE * 1.4426950408889634
NEG = -1e30
F32 = jnp.float32
BF = jnp.bfloat16
VM = pl.BlockSpec(memory_space=pltpu.VMEM)
SM = pl.BlockSpec(memory_space=pltpu.SMEM)
HB = pl.BlockSpec(memory_space=pl.ANY)
FAR = pl.BlockSpec(memory_space=pltpu.HBM)
ROW = (NQ, 1, TOK)
MAT = (NQ, HD, TOK)
EROW = (SH, 1, TOK)
EMAT = (SH, HD, TOK)


def S(shape, dt):
    return jax.ShapeDtypeStruct(shape, dt)


def call(kernel, name, outs, ins, scratch, args, keys, products, mib=16):
    mults = NQ * TOK * keys * HD * products
    return pl.pallas_call(
        kernel,
        out_shape=outs,
        in_specs=ins,
        out_specs=tuple(VM for _ in outs),
        scratch_shapes=scratch,
        compiler_params=pltpu.CompilerParams(vmem_limit_bytes=mib * 1024 * 1024),
        cost_estimate=pl.CostEstimate(
            flops=4 * mults, bytes_accessed=1_000_000, transcendentals=NQ * TOK * keys
        ),
        name=name,
    )(*args)


def dot(a, b):
    return jnp.dot(a, b, preferred_element_type=F32)


def pipeline(count, stages):
    held = [{} for _ in stages]
    for i in range(count + len(stages) - 1):
        for j, stage in enumerate(stages):
            t = i - j
            if 0 <= t < count:
                held[j][t] = stage(t, held[j - 1].pop(t) if j else None)


def start_loads(shards, kv, sems):
    copies = [
        pltpu.make_async_copy(s, kv.at[:, pl.ds(i * TOK, TOK), :], sems.at[i])
        for i, s in enumerate(shards)
    ]
    for c in copies:
        c.start()
    return copies


def chosen(refs, plan):
    return [refs[i] if j is None else refs[i].at[j] for i, j in plan]


PREFIX_PLAN = ((0, None), (1, None), (2, 0), (3, 0), (2, 1), (3, 1), (2, 2), (3, 2))
EACH = tuple((i, None) for i in range(8))


def causal():
    return lax.broadcasted_iota(jnp.int32, (TOK, TOK), 0) <= lax.broadcasted_iota(
        jnp.int32, (TOK, TOK), 1
    )


def forward(tasks, kv, q_ref, m_ref, l_ref, o_ref, mask=None):
    def scores(t, _):
        start, width, cols, hq, _h = tasks[t]
        s = dot(kv[0, pl.ds(start, width), cols], q_ref[hq])
        return s if mask is None else jnp.where(mask, s, NEG)

    def weigh(t, s):
        h = tasks[t][4]
        before = m_ref[h]
        top = jnp.maximum(before, jnp.max(s, axis=0, keepdims=True))
        p = jnp.exp2((s - top) * SC2)
        factor = jnp.exp2((before - top) * SC2)
        m_ref[h] = top
        l_ref[h] = l_ref[h] * factor + jnp.sum(p, axis=0, keepdims=True)
        return p.astype(BF), factor

    turned = {}

    def gather(t, item):
        start, width, cols, _hq, h = tasks[t]
        key = (t // SH, cols.start)
        if key not in turned:
            turned[key] = kv[1, pl.ds(start, width), cols].T
        o_ref[h] = o_ref[h] * item[1] + dot(turned[key], item[0])

    pipeline(len(tasks), [scores, weigh, gather])


def both_heads(start, width):
    return [
        (start, width, slice(e * HD, (e + 1) * HD), e * SH + g, e * SH + g)
        for e in range(NE)
        for g in range(SH)
    ]


def fwd_near_kernel(q_ref, mine, up_ref, *refs):
    m_ref, l_ref, o_ref, up_out, kv, sems, up_sem = refs[-7:]
    handed = pltpu.make_async_copy(up_ref, up_out, up_sem)
    handed.start()
    copies = start_loads((mine,), kv, sems)
    m_ref[...] = jnp.full(m_ref.shape, NEG, F32)
    l_ref[...] = jnp.zeros(l_ref.shape, F32)
    o_ref[...] = jnp.zeros(o_ref.shape, F32)
    copies[0].wait()
    forward(both_heads(0, TOK), kv, q_ref, m_ref, l_ref, o_ref, causal())
    handed.wait()


def fwd_far_kernel(x_ref, q_ref, m0, l0, o0, *refs, first, plan):
    pairs = len(plan) // 2
    shards, (m_ref, l_ref, o_ref, kv, sems) = chosen(refs, plan), refs[-5:]
    copies = start_loads(shards, kv, sems)
    m_ref[...] = m0[...]
    l_ref[...] = l0[...]
    o_ref[...] = o0[...]
    for c in copies:
        c.wait()

    def body(d, _):
        start = pl.multiple_of(d * 2 * TOK, 2 * TOK)
        forward(both_heads(start, 2 * TOK), kv, q_ref, m_ref, l_ref, o_ref)
        return 0

    lax.fori_loop(0, jnp.clip(x_ref[0] - first, 0, pairs), body, 0)
    if first:

        @pl.when(x_ref[1] == 1)
        def _():
            forward(both_heads(2 * pairs * TOK, TOK), kv, q_ref, m_ref, l_ref, o_ref)


def fwd_prefix_kernel(live_ref, q_ref, m0, l0, o0, *refs):
    shards, refs = chosen(refs, PREFIX_PLAN), refs[-8:]
    ot_ref, att_ref, lse_ref, kv, m_ref, l_ref, o_ref, sems = refs
    copies = start_loads(shards, kv, sems)
    m_ref[...] = m0[...]
    l_ref[...] = l0[...]
    o_ref[...] = o0[...]
    for c in copies:
        c.wait()
    width = 4 * TOK

    def body(i, _):
        forward(both_heads(pl.multiple_of(i * width, width), width), kv, q_ref, m_ref, l_ref, o_ref)
        return 0

    lax.fori_loop(0, 2, body, 0)
    live = live_ref[...]
    for h in range(NQ):
        total = l_ref[h]
        out = o_ref[h] * (live / total)
        ot_ref[h] = out.astype(BF)
        att_ref[:, h * HD : (h + 1) * HD] = out.T.astype(BF)
        lse_ref[h] = m_ref[h] * SC2 + jnp.log2(total)


def backward(tasks, kv, q_ref, qn_ref, g_ref, gn_ref, lse_ref, dl, dq, ps, ds, store, mask=None):
    def products(t, _):
        start, width, cols, h, _s, _b = tasks[t]
        return (
            dot(kv[0, pl.ds(start, width), cols], q_ref[h]),
            dot(kv[1, pl.ds(start, width), cols], g_ref[h]),
        )

    def weigh(t, item):
        _start, width, _cols, h, s, b = tasks[t]
        p = jnp.exp2(item[0] * SC2 - lse_ref[h])
        if mask is not None:
            p = jnp.where(mask, p, 0.0)
        d = (p * (item[1] - dl[s])).astype(BF)
        g = h % SH
        ps[b, :width, g * TOK : (g + 1) * TOK] = p.astype(BF)
        ds[b, :width, g * TOK : (g + 1) * TOK] = d
        return d

    turned = {}

    def apply(t, d):
        start, width, cols, h, s, b = tasks[t]
        key = (t // SH, cols.start)
        if key not in turned:
            turned[key] = kv[0, pl.ds(start, width), cols].T
        dq[s] += dot(turned[key], d)
        if h % SH == SH - 1:
            e = h // SH
            queries = qn_ref[e * SH : (e + 1) * SH].reshape(SH * TOK, HD)
            grads = gn_ref[e * SH : (e + 1) * SH].reshape(SH * TOK, HD)
            store(
                t,
                (dot(ds[b, :width], queries) * SCALE).astype(BF),
                dot(ps[b, :width], grads).astype(BF),
            )

    pipeline(len(tasks), [products, weigh, apply])


def deltas(g_ref, ot_ref, dl):
    for h in range(NQ):
        dl[h] = jnp.sum(g_ref[h].astype(F32) * ot_ref[h].astype(F32), axis=0, keepdims=True)


def bwd_prefix_kernel(q_ref, qn_ref, g_ref, gn_ref, ot_ref, lse_ref, *refs):
    shards, refs = chosen(refs, PREFIX_PLAN), refs[-8:]
    dq_ref, same, other, kv, dl, ps, ds, sems = refs
    copies = start_loads(shards, kv, sems)
    deltas(g_ref, ot_ref, dl)
    dq_ref[...] = jnp.zeros(dq_ref.shape, F32)
    for c in copies:
        c.wait()

    def body(d, _):
        local_backward(
            pl.multiple_of(d * 2 * TOK, 2 * TOK), 2 * TOK,
            (kv, q_ref, qn_ref, g_ref, gn_ref, lse_ref, dl, dq_ref, ps, ds),
            put_pair(same, other, d),
        )
        return 0

    lax.fori_loop(0, 4, body, 0)


def put_pair(same, other, d):
    def put(cols, dk, dv):
        for i, out in enumerate((same, other)):
            out[d, 0, :, cols] = dk[i * TOK : (i + 1) * TOK]
            out[d, 1, :, cols] = dv[i * TOK : (i + 1) * TOK]

    return put


def local_backward(start, width, refs, put, mask=None):
    kv, q_ref, qn_ref, g_ref, gn_ref, lse_ref, dl, dq, ps, ds = refs
    tasks = [
        (start, width, slice(e * HD, (e + 1) * HD), e * SH + g, e * SH + g, e)
        for e in range(NE)
        for g in range(SH)
    ]

    def store(t, dk, dv):
        e = t // SH
        put(slice(e * HD, (e + 1) * HD), dk, dv)

    backward(
        tasks, kv, q_ref, qn_ref, g_ref, gn_ref,
        lse_ref, dl, dq, ps, ds, store, mask,
    )


def bwd_local_kernel(x_ref, q_ref, qn_ref, g_ref, gn_ref, ot_ref, lse_ref, dq0, *refs, late):
    shards, refs = refs[:4], refs[-9:]
    out_ref, same, other, kv, dl, dq_ref, ps, ds, sems = refs
    copies = start_loads(shards, kv, sems)
    deltas(g_ref, ot_ref, dl)
    dq_ref[...] = dq0[...]
    for c in copies:
        c.wait()
    shared = (kv, q_ref, qn_ref, g_ref, gn_ref, lse_ref, dl, dq_ref, ps, ds)
    x, core = x_ref[0], x_ref[1]
    skipped = 2 if late else 0

    def put_to(out):
        def put(cols, dk, dv):
            out[0, 0, :, cols] = dk
            out[0, 1, :, cols] = dv

        return put

    if not late:
        local_backward(0, TOK, shared, put_to(same), causal())

        @pl.when(core == 1)
        def _():
            local_backward(TOK, TOK, shared, put_to(other))

        @pl.when(core == 0)
        def _():
            other[0] = jnp.zeros(other.shape[1:], BF)

    def body(d, _):
        start = pl.multiple_of(d * 2 * TOK, 2 * TOK)
        local_backward(start, 2 * TOK, shared, put_pair(same, other, d))
        return 0

    stop = jnp.clip(x + 1 - skipped, 0 if late else 1, 2)
    lax.fori_loop(0 if late else 1, stop, body, 0)

    def blank(d, _):
        same[d] = jnp.zeros(same.shape[1:], BF)
        other[d] = jnp.zeros(other.shape[1:], BF)
        return 0

    lax.fori_loop(stop, 2, blank, 0)
    if not late:
        out_ref[...] = dq_ref[...]
        return
    for h in range(NQ):
        out_ref[:, h * HD : (h + 1) * HD] = (dq_ref[h] * SCALE).T.astype(BF)


def dma(*n):
    return pltpu.SemaphoreType.DMA(n)


def kv_scratch(keys, cols):
    return pltpu.VMEM((2, keys, cols), BF)


PAIR = (2, TOK, NE * HD)
HALF = (2, TOK, HD)


def fwd_near(qt, mine, up, *after):
    return call(
        fwd_near_kernel, "fwd_near",
        (S(ROW, F32), S(ROW, F32), S(MAT, F32), S(up.shape, BF)),
        [VM, HB, HB] + [HB] * len(after),
        [kv_scratch(TOK, NE * HD), dma(1), pltpu.SemaphoreType.DMA],
        (qt, mine, up, *after), 256, 2,
    )


def fwd_far(xc, qt, state, shards, plan, first, *after):
    n = len(plan)
    return call(
        functools.partial(fwd_far_kernel, first=first, plan=plan), "fwd_far",
        (S(ROW, F32), S(ROW, F32), S(MAT, F32)),
        [SM] + [VM] * 4 + [HB] * (len(shards) + len(after)),
        [kv_scratch(n * TOK, NE * HD), dma(n)], (xc, qt, *state, *shards, *after), 256 * n, 2,
    )


def fwd_prefix(live, qt, state, shards, *after):
    return call(
        fwd_prefix_kernel, "fwd_prefix", (S(MAT, BF), S((TOK, NQ * HD), BF), S(ROW, F32)),
        [VM] * 5 + [HB] * (4 + len(after)),
        [
            kv_scratch(8 * TOK, NE * HD), pltpu.VMEM(ROW, F32), pltpu.VMEM(ROW, F32),
            pltpu.VMEM(MAT, F32), dma(8),
        ],
        (live, qt, *state, *shards, *after), 2048, 2,
    )


def bwd_scratch(keys, width):
    return (
        [kv_scratch(keys, NE * HD), pltpu.VMEM(ROW, F32)]
        + [pltpu.VMEM((2, width, SH * TOK), BF)] * 2
        + [dma(keys // TOK)]
    )


def bwd_prefix(args, shards, *after):
    part = (4,) + PAIR
    return call(
        bwd_prefix_kernel, "bwd_prefix", (S(MAT, F32), S(part, BF), S(part, BF)),
        [VM] * 6 + [HB] * (4 + len(after)), bwd_scratch(8 * TOK, 2 * TOK),
        (*args, *shards, *after), 2048, 5,
    )


def bwd_local(xc, args, dq, shards, late, *after):
    part = (2,) + PAIR
    scratch = bwd_scratch(4 * TOK, 2 * TOK)
    return call(
        functools.partial(bwd_local_kernel, late=late), "bwd_local",
        (S((TOK, NQ * HD), BF) if late else S(MAT, F32), S(part, BF), S(part, BF)),
        [SM] + [VM] * 7 + [HB] * (4 + len(after)),
        scratch[:2] + [pltpu.VMEM(MAT, F32)] + scratch[2:],
        (xc, *args, dq, *shards, *after), 1024, 5,
    )


def run_copies(pairs, sems):
    copies = [pltpu.make_async_copy(a, b, sems.at[i]) for i, (a, b) in enumerate(pairs)]
    for c in copies:
        c.start()
    return copies


def stack_kernel(k_ref, v_ref, out_ref, sems):
    for c in run_copies([(k_ref.at[0], out_ref.at[0]), (v_ref.at[0], out_ref.at[1])], sems):
        c.wait()


def stack_pair(k, v):
    return call(
        stack_kernel, "stack_pair", (S(PAIR, BF),), [FAR, FAR], [dma(2)], (k, v), 8, 1
    )[0]


def merge_kernel(*refs):
    out_ref, sems = refs[-2:]
    for c in run_copies([(refs[i], out_ref.at[i]) for i in range(3)], sems):
        c.wait()


def merge(parts, *after):
    return call(
        merge_kernel, "merge", (S((3,) + PAIR, BF),), [HB] * (3 + len(after)), [dma(3)],
        (*parts, *after), 8, 1,
    )[0]


def pick_kernel(index_ref, *refs):
    spread, outs, sems = refs[:4], refs[-3:-1], refs[-1]
    for o, out in enumerate(outs):
        for i, piece in enumerate(spread):

            @pl.when(index_ref[o] == i)
            def _():
                pltpu.make_async_copy(piece, out, sems.at[o]).start()

    for o, out in enumerate(outs):
        pltpu.make_async_copy(spread[0], out, sems.at[o]).wait()


def pick(indices, options, *after):
    return call(
        pick_kernel, "pick", (S(PAIR, BF),) * 2, [SM] + [HB] * (4 + len(after)), [dma(2)],
        (indices.astype(jnp.int32), *options, *after), 8, 1,
    )


def add_pairs_kernel(a_ref, b_ref, *refs, count):
    outs = refs[-count:]
    for d in range(count):
        outs[d][...] = (a_ref[d].astype(F32) + b_ref[d].astype(F32)).astype(BF)


def add_pairs(a, b, *after):
    n = a.shape[0]
    return call(
        functools.partial(add_pairs_kernel, count=n), "add_pairs", (S(PAIR, BF),) * n,
        [VM, VM] + [HB] * len(after), [], (a, b, *after), 8, 1,
    )


def add_all_kernel(*refs, count):
    total = refs[0][...].astype(F32)
    for ref in refs[1:count]:
        total = total + ref[...].astype(F32)
    refs[-1][...] = total.astype(BF)


def add_all(parts, *after):
    return call(
        functools.partial(add_all_kernel, count=len(parts)), "add_all", (S(PAIR, BF),),
        [VM] * len(parts) + [HB] * len(after), [], (*parts, *after), 8, 1,
    )[0]


def slot_kernel(flag_ref, a_ref, b_ref, *refs):
    a = a_ref[...].astype(F32)
    b = b_ref[...].astype(F32)
    for d, out in enumerate(refs[-4:]):
        out[...] = (
            jnp.where(flag_ref[d] == 1, a, 0.0) + jnp.where(flag_ref[4 + d] == 1, b, 0.0)
        ).astype(BF)


def slots(flags, a, b, *after):
    return call(
        slot_kernel, "slots", (S(PAIR, BF),) * 4, [SM, VM, VM] + [HB] * len(after), [],
        (flags, a, b, *after), 8, 1,
    )


def turn_kernel(q_ref, k_ref, v_ref, _first, *refs):
    qt_ref, qn_ref, pair_ref, q, sems = refs[-5:]
    copies = run_copies(
        [(q_ref.at[0], q), (k_ref.at[0], pair_ref.at[0]), (v_ref.at[0], pair_ref.at[1])], sems
    )
    copies[0].wait()
    for h in range(NQ):
        block = q[:, h * HD : (h + 1) * HD]
        qn_ref[h] = block
        qt_ref[h] = block.T
    copies[1].wait()
    copies[2].wait()


def turn(q, k, v, first):
    return call(
        turn_kernel, "turn", (S(MAT, BF), S((NQ, TOK, HD), BF), S(PAIR, BF)), [FAR] * 3 + [HB],
        [pltpu.VMEM((TOK, NQ * HD), BF), dma(3)], (q, k, v, first), 8, 1,
    )


def back_kernel(col_ref, w_ref, up_ref, *refs, last):
    w, sems = refs[-2:]
    half = up_ref.shape[1]
    rows = 2 * HD
    copies = []
    for i in range(NQ // 2):
        block = w_ref.at[pl.ds(i * rows, rows), pl.ds(pl.multiple_of(col_ref[0] * half, half), half)]
        copies.append(pltpu.make_async_copy(block, w.at[i], sems.at[i]))
        copies[-1].start()
    turned = up_ref[...].T
    for i, c in enumerate(copies):
        c.wait()
        acc = dot(w[i], turned)
        if not last:
            refs[-3][i * rows : (i + 1) * rows] = acc
            continue
        first_ref, row_ref = refs[:2]
        gt_ref, gn_ref = refs[-4:-2]
        out = ((first_ref[i * rows : (i + 1) * rows] + acc) * row_ref[...]).astype(BF)
        for j in range(2):
            gt_ref[2 * i + j] = out[j * HD : (j + 1) * HD]
            gn_ref[2 * i + j] = out[j * HD : (j + 1) * HD].T


def back_part(col, w, up, more=(), after=()):
    half = up.shape[1]
    outs = (S(MAT, BF), S((NQ, TOK, HD), BF)) if more else (S((NQ * HD, TOK), F32),)
    return call(
        functools.partial(back_kernel, last=bool(more)), "back_part", outs,
        [SM, FAR, VM] + [VM] * len(more) + [HB] * len(after),
        [pltpu.VMEM((NQ // 2, 2 * HD, half), BF), dma(NQ // 2)],
        (col, w, up, *more, *after), 1280, 1, 16 if more else 52,
    )


def mix_kernel(col_ref, a_ref, w_ref, *refs, last):
    out_ref, w, sems = refs[-3:]
    half = out_ref.shape[1]
    steps, _, width = w.shape
    copies = []
    for i in range(steps):
        first = pl.multiple_of(col_ref[0] * half + i * width, width)
        copies.append(pltpu.make_async_copy(w_ref.at[:, pl.ds(first, width)], w.at[i], sems.at[i]))
        copies[-1].start()
    a = a_ref[...]
    for i, c in enumerate(copies):
        c.wait()
        cols = slice(i * width, (i + 1) * width)
        acc = dot(a, w[i])
        if last:
            acc = acc + refs[0][:, cols].astype(F32)
        out_ref[:, cols] = acc.astype(BF)


def mix_part(col, att, w, more=(), after=()):
    half = w.shape[1] // 2
    width = 512
    return call(
        functools.partial(mix_kernel, last=bool(more)), "mix_part", (S((TOK, half), BF),),
        [SM, VM, FAR] + [VM] * len(more) + [HB] * len(after),
        [pltpu.VMEM((half // width, NQ * HD, width), BF), dma(half // width)],
        (col, att, w, *more, *after), 1280, 1, 52 if more else 16,
    )[0]


def shift(d, swap=0):
    return [(x * 2 + c, ((x + d) % 4) * 2 + (c ^ swap)) for x in range(4) for c in range(2)]


SWAP = shift(0, 1)


def shards(
    queries, keys, values, prefix_keys, prefix_values, rollout_group, roll_length, advantage,
    upstream, w_out,
):
    ctx = lax.axis_index("ctx")
    grp = lax.axis_index("grp")
    tp = lax.axis_index("tp")
    x, core = ctx // 2, ctx % 2
    z, ylo = grp // 2, grp % 2
    xc = jnp.stack([x, core]).astype(jnp.int32)
    own_col = tp.reshape(1).astype(jnp.int32)
    other_col = 1 - own_col
    group = rollout_group[0]
    mate = lax.ppermute(rollout_group, "grp", SWAP)[0]
    positions = ctx * TOK + lax.iota(jnp.int32, TOK)
    live = (positions < roll_length[0]).astype(F32)[None]
    row = live * advantage[0]

    prefix = stack_pair(prefix_keys, prefix_values)
    spread = [prefix] + [lax.ppermute(prefix, "grp", shift(d)) for d in (1, 2, 3)]
    first = back_part(own_col, w_out, upstream[0])[0]
    qt, qn, local = turn(queries, keys, values, first)
    local_same = [lax.ppermute(local, "ctx", shift(d)) for d in (1, 2, 3)]
    local_mate, *mates = [lax.ppermute(s, "ctx", SWAP) for s in (local, *local_same)]
    pairs = [s for pair in zip(local_same, mates) for s in pair]

    places = jnp.stack([(z - mate // 2) % 4, (z - group // 2) % 4])
    sent, held = pick(places, spread, qt)
    came = lax.ppermute(sent, "grp", SWAP)
    *state, up = fwd_near(qt, local, upstream[0], sent)
    up_other = lax.ppermute(up, "tp", [(0, 1), (1, 0)])
    own = jnp.where(group % 2 == ylo, held, came)
    own_mate = lax.ppermute(own, "ctx", SWAP)
    own_same = [lax.ppermute(own, "ctx", shift(d)) for d in (1, 2, 3)]
    state = fwd_far(xc, qt, state, pairs[:4], EACH[:4], 0, *pairs[4:])
    merged = merge(own_same, state[0])
    own_mates = lax.ppermute(merged, "ctx", SWAP)
    state = fwd_far(xc, qt, state, [*pairs[4:], local_mate], EACH[:3], 2, merged)
    prefix_shards = [own, own_mate, merged, own_mates]
    ot, att, lse = fwd_prefix(live, qt, state, prefix_shards)
    half = mix_part(other_col, att, w_out)
    mix_other = lax.ppermute(half, "tp", [(0, 1), (1, 0)])
    gt, gn = back_part(other_col, w_out, up_other, (first, row), (half,))
    args = (qt, qn, gt, gn, ot, lse)

    dq, same, other = bwd_prefix(args, prefix_shards)
    got = lax.ppermute(other, "ctx", SWAP)
    sums = add_pairs(same, got)
    moved = [lax.ppermute(sums[d], "ctx", shift(-d)) for d in (1, 2, 3)]
    dq, early_same, early_other = bwd_local(
        xc, args, dq, [local, local_mate, *pairs[:2]], False, sums[0], mix_other
    )
    column = add_all([sums[0]] + moved, dq)
    theirs = lax.ppermute(column, "grp", SWAP)
    grad_queries, late_same, late_other = bwd_local(xc, args, dq, pairs[2:], True, column)
    target = (z + lax.iota(jnp.int32, 4)) % 4
    flags = jnp.concatenate(
        [(g % 2 == ylo) & (g // 2 == target) for g in (group, mate)]
    ).astype(jnp.int32)
    placed = slots(flags, column, theirs, late_same)
    arrived = [lax.ppermute(placed[d], "grp", shift(d)) for d in (1, 2, 3)]
    early = add_pairs(early_same, lax.ppermute(early_other, "ctx", SWAP), placed[0])
    late = add_pairs(late_same, lax.ppermute(late_other, "ctx", SWAP), placed[0])
    sent_back = [lax.ppermute(p, "ctx", shift(-d)) for d, p in ((1, early[1]), (2, late[0]), (3, late[1]))]
    mixed = mix_part(own_col, att, w_out, (mix_other,), (late[0],))
    owned = add_all([placed[0]] + arrived)
    mine = add_all([early[0]] + sent_back)
    return (
        att[None],
        mixed[None],
        grad_queries[None],
        mine[0][None],
        mine[1][None],
        owned[0][None],
        owned[1][None],
    )


def solution(mesh):
    spec = P("grp", "ctx", "tp")
    in_specs = (spec,) * 5 + (P("grp"),) * 3 + (spec, P("tp", None))
    return jax.shard_map(
        shards, mesh=mesh, in_specs=in_specs, out_specs=(spec,) * 7, check_vma=False
    )
```

```python
import functools

import jax
import jax.numpy as jnp
from jax import lax
from jax.experimental import pallas as pl
from jax.experimental.pallas import tpu as pltpu
from jax.sharding import PartitionSpec as P

HD = 128
TOK = 256
NQ = 10
NE = 2
SH = 5
SCALE = HD ** (-0.5)
SC2 = SCALE * 1.4426950408889634
NEG = -1e30
F32 = jnp.float32
BF = jnp.bfloat16
VM = pl.BlockSpec(memory_space=pltpu.VMEM)
SM = pl.BlockSpec(memory_space=pltpu.SMEM)
HB = pl.BlockSpec(memory_space=pl.ANY)
FAR = pl.BlockSpec(memory_space=pltpu.HBM)
ROW = (NQ, 1, TOK)
MAT = (NQ, HD, TOK)
EROW = (SH, 1, TOK)
EMAT = (SH, HD, TOK)


def S(shape, dt):
    return jax.ShapeDtypeStruct(shape, dt)


def call(kernel, name, outs, ins, scratch, args, keys, products, mib=16):
    mults = NQ * TOK * keys * HD * products
    return pl.pallas_call(
        kernel,
        out_shape=outs,
        in_specs=ins,
        out_specs=tuple(VM for _ in outs),
        scratch_shapes=scratch,
        compiler_params=pltpu.CompilerParams(vmem_limit_bytes=mib * 1024 * 1024),
        cost_estimate=pl.CostEstimate(
            flops=4 * mults, bytes_accessed=1_000_000, transcendentals=NQ * TOK * keys
        ),
        name=name,
    )(*args)


def dot(a, b):
    return jnp.dot(a, b, preferred_element_type=F32)


def pipeline(count, stages):
    held = [{} for _ in stages]
    for i in range(count + len(stages) - 1):
        for j, stage in enumerate(stages):
            t = i - j
            if 0 <= t < count:
                held[j][t] = stage(t, held[j - 1].pop(t) if j else None)


def start_loads(shards, kv, sems):
    copies = [
        pltpu.make_async_copy(s, kv.at[:, pl.ds(i * TOK, TOK), :], sems.at[i])
        for i, s in enumerate(shards)
    ]
    for c in copies:
        c.start()
    return copies


def chosen(refs, plan):
    return [refs[i] if j is None else refs[i].at[j] for i, j in plan]


PREFIX_PLAN = ((0, None), (1, None), (2, 0), (3, 0), (2, 1), (3, 1), (2, 2), (3, 2))
EACH = tuple((i, None) for i in range(8))


def causal():
    return lax.broadcasted_iota(jnp.int32, (TOK, TOK), 0) <= lax.broadcasted_iota(
        jnp.int32, (TOK, TOK), 1
    )


def forward(tasks, kv, q_ref, m_ref, l_ref, o_ref, mask=None):
    def scores(t, _):
        start, width, cols, hq, _h = tasks[t]
        s = dot(kv[0, pl.ds(start, width), cols], q_ref[hq])
        return s if mask is None else jnp.where(mask, s, NEG)

    def weigh(t, s):
        h = tasks[t][4]
        before = m_ref[h]
        top = jnp.maximum(before, jnp.max(s, axis=0, keepdims=True))
        p = jnp.exp2((s - top) * SC2)
        factor = jnp.exp2((before - top) * SC2)
        m_ref[h] = top
        l_ref[h] = l_ref[h] * factor + jnp.sum(p, axis=0, keepdims=True)
        return p.astype(BF), factor

    turned = {}

    def gather(t, item):
        start, width, cols, _hq, h = tasks[t]
        key = (t // SH, cols.start)
        if key not in turned:
            turned[key] = kv[1, pl.ds(start, width), cols].T
        o_ref[h] = o_ref[h] * item[1] + dot(turned[key], item[0])

    pipeline(len(tasks), [scores, weigh, gather])


def both_heads(start, width):
    return [
        (start, width, slice(e * HD, (e + 1) * HD), e * SH + g, e * SH + g)
        for e in range(NE)
        for g in range(SH)
    ]


def fwd_near_kernel(q_ref, mine, up_ref, *refs):
    m_ref, l_ref, o_ref, up_out, kv, sems, up_sem = refs[-7:]
    handed = pltpu.make_async_copy(up_ref, up_out, up_sem)
    handed.start()
    copies = start_loads((mine,), kv, sems)
    m_ref[...] = jnp.full(m_ref.shape, NEG, F32)
    l_ref[...] = jnp.zeros(l_ref.shape, F32)
    o_ref[...] = jnp.zeros(o_ref.shape, F32)
    copies[0].wait()
    forward(both_heads(0, TOK), kv, q_ref, m_ref, l_ref, o_ref, causal())
    handed.wait()


def fwd_far_kernel(x_ref, q_ref, m0, l0, o0, *refs, first, plan):
    pairs = len(plan) // 2
    shards, (m_ref, l_ref, o_ref, kv, sems) = chosen(refs, plan), refs[-5:]
    copies = start_loads(shards, kv, sems)
    m_ref[...] = m0[...]
    l_ref[...] = l0[...]
    o_ref[...] = o0[...]
    for c in copies:
        c.wait()

    def body(d, _):
        start = pl.multiple_of(d * 2 * TOK, 2 * TOK)
        forward(both_heads(start, 2 * TOK), kv, q_ref, m_ref, l_ref, o_ref)
        return 0

    lax.fori_loop(0, jnp.clip(x_ref[0] - first, 0, pairs), body, 0)
    if first:

        @pl.when(x_ref[1] == 1)
        def _():
            forward(both_heads(2 * pairs * TOK, TOK), kv, q_ref, m_ref, l_ref, o_ref)


def fwd_prefix_kernel(live_ref, q_ref, m0, l0, o0, *refs):
    shards, refs = chosen(refs, PREFIX_PLAN), refs[-8:]
    ot_ref, att_ref, lse_ref, kv, m_ref, l_ref, o_ref, sems = refs
    copies = start_loads(shards, kv, sems)
    m_ref[...] = m0[...]
    l_ref[...] = l0[...]
    o_ref[...] = o0[...]
    for c in copies:
        c.wait()
    width = 4 * TOK

    def body(i, _):
        forward(both_heads(pl.multiple_of(i * width, width), width), kv, q_ref, m_ref, l_ref, o_ref)
        return 0

    lax.fori_loop(0, 2, body, 0)
    live = live_ref[...]
    for h in range(NQ):
        total = l_ref[h]
        out = o_ref[h] * (live / total)
        ot_ref[h] = out.astype(BF)
        att_ref[:, h * HD : (h + 1) * HD] = out.T.astype(BF)
        lse_ref[h] = m_ref[h] * SC2 + jnp.log2(total)


def backward(tasks, kv, q_ref, qn_ref, g_ref, gn_ref, lse_ref, dl, dq, ps, ds, store, mask=None):
    def products(t, _):
        start, width, cols, h, _s, _b = tasks[t]
        return (
            dot(kv[0, pl.ds(start, width), cols], q_ref[h]),
            dot(kv[1, pl.ds(start, width), cols], g_ref[h]),
        )

    def weigh(t, item):
        _start, width, _cols, h, s, b = tasks[t]
        p = jnp.exp2(item[0] * SC2 - lse_ref[h])
        if mask is not None:
            p = jnp.where(mask, p, 0.0)
        d = (p * (item[1] - dl[s])).astype(BF)
        g = h % SH
        ps[b, :width, g * TOK : (g + 1) * TOK] = p.astype(BF)
        ds[b, :width, g * TOK : (g + 1) * TOK] = d
        return d

    turned = {}

    def apply(t, d):
        start, width, cols, h, s, b = tasks[t]
        key = (t // SH, cols.start)
        if key not in turned:
            turned[key] = kv[0, pl.ds(start, width), cols].T
        dq[s] += dot(turned[key], d)
        if h % SH == SH - 1:
            e = h // SH
            queries = qn_ref[e * SH : (e + 1) * SH].reshape(SH * TOK, HD)
            grads = gn_ref[e * SH : (e + 1) * SH].reshape(SH * TOK, HD)
            store(
                t,
                (dot(ds[b, :width], queries) * SCALE).astype(BF),
                dot(ps[b, :width], grads).astype(BF),
            )

    pipeline(len(tasks), [products, weigh, apply])


def deltas(g_ref, ot_ref, dl):
    for h in range(NQ):
        dl[h] = jnp.sum(g_ref[h].astype(F32) * ot_ref[h].astype(F32), axis=0, keepdims=True)


def bwd_prefix_kernel(q_ref, qn_ref, g_ref, gn_ref, ot_ref, lse_ref, *refs):
    shards, refs = chosen(refs, PREFIX_PLAN), refs[-8:]
    dq_ref, same, other, kv, dl, ps, ds, sems = refs
    copies = start_loads(shards, kv, sems)
    deltas(g_ref, ot_ref, dl)
    dq_ref[...] = jnp.zeros(dq_ref.shape, F32)
    for c in copies:
        c.wait()

    def body(d, _):
        local_backward(
            pl.multiple_of(d * 2 * TOK, 2 * TOK), 2 * TOK,
            (kv, q_ref, qn_ref, g_ref, gn_ref, lse_ref, dl, dq_ref, ps, ds),
            put_pair(same, other, d),
        )
        return 0

    lax.fori_loop(0, 4, body, 0)


def put_pair(same, other, d):
    def put(cols, dk, dv):
        for i, out in enumerate((same, other)):
            out[d, 0, :, cols] = dk[i * TOK : (i + 1) * TOK]
            out[d, 1, :, cols] = dv[i * TOK : (i + 1) * TOK]

    return put


def local_backward(start, width, refs, put, mask=None):
    kv, q_ref, qn_ref, g_ref, gn_ref, lse_ref, dl, dq, ps, ds = refs
    tasks = [
        (start, width, slice(e * HD, (e + 1) * HD), e * SH + g, e * SH + g, e)
        for e in range(NE)
        for g in range(SH)
    ]

    def store(t, dk, dv):
        e = t // SH
        put(slice(e * HD, (e + 1) * HD), dk, dv)

    backward(
        tasks, kv, q_ref, qn_ref, g_ref, gn_ref,
        lse_ref, dl, dq, ps, ds, store, mask,
    )


def bwd_local_kernel(x_ref, q_ref, qn_ref, g_ref, gn_ref, ot_ref, lse_ref, dq0, *refs, late):
    shards, refs = refs[:4], refs[-9:]
    out_ref, same, other, kv, dl, dq_ref, ps, ds, sems = refs
    copies = start_loads(shards, kv, sems)
    deltas(g_ref, ot_ref, dl)
    dq_ref[...] = dq0[...]
    for c in copies:
        c.wait()
    shared = (kv, q_ref, qn_ref, g_ref, gn_ref, lse_ref, dl, dq_ref, ps, ds)
    x, core = x_ref[0], x_ref[1]
    skipped = 2 if late else 0

    def put_to(out):
        def put(cols, dk, dv):
            out[0, 0, :, cols] = dk
            out[0, 1, :, cols] = dv

        return put

    if not late:
        local_backward(0, TOK, shared, put_to(same), causal())

        @pl.when(core == 1)
        def _():
            local_backward(TOK, TOK, shared, put_to(other))

        @pl.when(core == 0)
        def _():
            other[0] = jnp.zeros(other.shape[1:], BF)

    def body(d, _):
        start = pl.multiple_of(d * 2 * TOK, 2 * TOK)
        local_backward(start, 2 * TOK, shared, put_pair(same, other, d))
        return 0

    stop = jnp.clip(x + 1 - skipped, 0 if late else 1, 2)
    lax.fori_loop(0 if late else 1, stop, body, 0)

    def blank(d, _):
        same[d] = jnp.zeros(same.shape[1:], BF)
        other[d] = jnp.zeros(other.shape[1:], BF)
        return 0

    lax.fori_loop(stop, 2, blank, 0)
    if not late:
        out_ref[...] = dq_ref[...]
        return
    for h in range(NQ):
        out_ref[:, h * HD : (h + 1) * HD] = (dq_ref[h] * SCALE).T.astype(BF)


def dma(*n):
    return pltpu.SemaphoreType.DMA(n)


def kv_scratch(keys, cols):
    return pltpu.VMEM((2, keys, cols), BF)


PAIR = (2, TOK, NE * HD)
HALF = (2, TOK, HD)


def fwd_near(qt, mine, up, *after):
    return call(
        fwd_near_kernel, "fwd_near",
        (S(ROW, F32), S(ROW, F32), S(MAT, F32), S(up.shape, BF)),
        [VM, HB, HB] + [HB] * len(after),
        [kv_scratch(TOK, NE * HD), dma(1), pltpu.SemaphoreType.DMA],
        (qt, mine, up, *after), 256, 2,
    )


def fwd_far(xc, qt, state, shards, plan, first, *after):
    n = len(plan)
    return call(
        functools.partial(fwd_far_kernel, first=first, plan=plan), "fwd_far",
        (S(ROW, F32), S(ROW, F32), S(MAT, F32)),
        [SM] + [VM] * 4 + [HB] * (len(shards) + len(after)),
        [kv_scratch(n * TOK, NE * HD), dma(n)], (xc, qt, *state, *shards, *after), 256 * n, 2,
    )


def fwd_prefix(live, qt, state, shards, *after):
    return call(
        fwd_prefix_kernel, "fwd_prefix", (S(MAT, BF), S((TOK, NQ * HD), BF), S(ROW, F32)),
        [VM] * 5 + [HB] * (4 + len(after)),
        [
            kv_scratch(8 * TOK, NE * HD), pltpu.VMEM(ROW, F32), pltpu.VMEM(ROW, F32),
            pltpu.VMEM(MAT, F32), dma(8),
        ],
        (live, qt, *state, *shards, *after), 1024, 2,
    )


def bwd_scratch(keys, width):
    return (
        [kv_scratch(keys, NE * HD), pltpu.VMEM(ROW, F32)]
        + [pltpu.VMEM((2, width, SH * TOK), BF)] * 2
        + [dma(keys // TOK)]
    )


def bwd_prefix(args, shards, *after):
    part = (4,) + PAIR
    return call(
        bwd_prefix_kernel, "bwd_prefix", (S(MAT, F32), S(part, BF), S(part, BF)),
        [VM] * 6 + [HB] * (4 + len(after)), bwd_scratch(8 * TOK, 2 * TOK),
        (*args, *shards, *after), 2048, 5,
    )


def bwd_local(xc, args, dq, shards, late, *after):
    part = (2,) + PAIR
    scratch = bwd_scratch(4 * TOK, 2 * TOK)
    return call(
        functools.partial(bwd_local_kernel, late=late), "bwd_local",
        (S((TOK, NQ * HD), BF) if late else S(MAT, F32), S(part, BF), S(part, BF)),
        [SM] + [VM] * 7 + [HB] * (4 + len(after)),
        scratch[:2] + [pltpu.VMEM(MAT, F32)] + scratch[2:],
        (xc, *args, dq, *shards, *after), 1024, 5,
    )


def run_copies(pairs, sems):
    copies = [pltpu.make_async_copy(a, b, sems.at[i]) for i, (a, b) in enumerate(pairs)]
    for c in copies:
        c.start()
    return copies


def stack_kernel(k_ref, v_ref, out_ref, sems):
    for c in run_copies([(k_ref.at[0], out_ref.at[0]), (v_ref.at[0], out_ref.at[1])], sems):
        c.wait()


def stack_pair(k, v):
    return call(
        stack_kernel, "stack_pair", (S(PAIR, BF),), [FAR, FAR], [dma(2)], (k, v), 8, 1
    )[0]


def merge_kernel(*refs):
    out_ref, sems = refs[-2:]
    for c in run_copies([(refs[i], out_ref.at[i]) for i in range(3)], sems):
        c.wait()


def merge(parts, *after):
    return call(
        merge_kernel, "merge", (S((3,) + PAIR, BF),), [HB] * (3 + len(after)), [dma(3)],
        (*parts, *after), 8, 1,
    )[0]


def pick_kernel(index_ref, *refs):
    spread, outs, sems = refs[:4], refs[-3:-1], refs[-1]
    for o, out in enumerate(outs):
        for i, piece in enumerate(spread):

            @pl.when(index_ref[o] == i)
            def _():
                pltpu.make_async_copy(piece, out, sems.at[o]).start()

    for o, out in enumerate(outs):
        pltpu.make_async_copy(spread[0], out, sems.at[o]).wait()


def pick(indices, options, *after):
    return call(
        pick_kernel, "pick", (S(PAIR, BF),) * 2, [SM] + [HB] * (4 + len(after)), [dma(2)],
        (indices.astype(jnp.int32), *options, *after), 8, 1,
    )


def add_pairs_kernel(a_ref, b_ref, *refs, count):
    outs = refs[-count:]
    for d in range(count):
        outs[d][...] = (a_ref[d].astype(F32) + b_ref[d].astype(F32)).astype(BF)


def add_pairs(a, b, *after):
    n = a.shape[0]
    return call(
        functools.partial(add_pairs_kernel, count=n), "add_pairs", (S(PAIR, BF),) * n,
        [VM, VM] + [HB] * len(after), [], (a, b, *after), 8, 1,
    )


def add_all_kernel(*refs, count):
    total = refs[0][...].astype(F32)
    for ref in refs[1:count]:
        total = total + ref[...].astype(F32)
    refs[-1][...] = total.astype(BF)


def add_all(parts, *after):
    return call(
        functools.partial(add_all_kernel, count=len(parts)), "add_all", (S(PAIR, BF),),
        [VM] * len(parts) + [HB] * len(after), [], (*parts, *after), 8, 1,
    )[0]


def slot_kernel(flag_ref, a_ref, b_ref, *refs):
    a = a_ref[...].astype(F32)
    b = b_ref[...].astype(F32)
    for d, out in enumerate(refs[-4:]):
        out[...] = (
            jnp.where(flag_ref[d] == 1, a, 0.0) + jnp.where(flag_ref[4 + d] == 1, b, 0.0)
        ).astype(BF)


def slots(flags, a, b, *after):
    return call(
        slot_kernel, "slots", (S(PAIR, BF),) * 4, [SM, VM, VM] + [HB] * len(after), [],
        (flags, a, b, *after), 8, 1,
    )


def turn_kernel(q_ref, k_ref, v_ref, _first, *refs):
    qt_ref, qn_ref, pair_ref, q, sems = refs[-5:]
    copies = run_copies(
        [(q_ref.at[0], q), (k_ref.at[0], pair_ref.at[0]), (v_ref.at[0], pair_ref.at[1])], sems
    )
    copies[0].wait()
    for h in range(NQ):
        block = q[:, h * HD : (h + 1) * HD]
        qn_ref[h] = block
        qt_ref[h] = block.T
    copies[1].wait()
    copies[2].wait()


def turn(q, k, v, first):
    return call(
        turn_kernel, "turn", (S(MAT, BF), S((NQ, TOK, HD), BF), S(PAIR, BF)), [FAR] * 3 + [HB],
        [pltpu.VMEM((TOK, NQ * HD), BF), dma(3)], (q, k, v, first), 8, 1,
    )


def back_kernel(col_ref, w_ref, up_ref, *refs, last):
    w, sems = refs[-2:]
    half = up_ref.shape[1]
    rows = 2 * HD
    copies = []
    for i in range(NQ // 2):
        block = w_ref.at[pl.ds(i * rows, rows), pl.ds(pl.multiple_of(col_ref[0] * half, half), half)]
        copies.append(pltpu.make_async_copy(block, w.at[i], sems.at[i]))
        copies[-1].start()
    turned = up_ref[...].T
    for i, c in enumerate(copies):
        c.wait()
        acc = dot(w[i], turned)
        if not last:
            refs[-3][i * rows : (i + 1) * rows] = acc
            continue
        first_ref, row_ref = refs[:2]
        gt_ref, gn_ref = refs[-4:-2]
        out = ((first_ref[i * rows : (i + 1) * rows] + acc) * row_ref[...]).astype(BF)
        for j in range(2):
            gt_ref[2 * i + j] = out[j * HD : (j + 1) * HD]
            gn_ref[2 * i + j] = out[j * HD : (j + 1) * HD].T


def back_part(col, w, up, more=(), after=()):
    half = up.shape[1]
    outs = (S(MAT, BF), S((NQ, TOK, HD), BF)) if more else (S((NQ * HD, TOK), F32),)
    return call(
        functools.partial(back_kernel, last=bool(more)), "back_part", outs,
        [SM, FAR, VM] + [VM] * len(more) + [HB] * len(after),
        [pltpu.VMEM((NQ // 2, 2 * HD, half), BF), dma(NQ // 2)],
        (col, w, up, *more, *after), 1280, 1, 16 if more else 52,
    )


def mix_kernel(col_ref, a_ref, w_ref, *refs, last):
    out_ref, w, sems = refs[-3:]
    half = out_ref.shape[1]
    steps, _, width = w.shape
    copies = []
    for i in range(steps):
        first = pl.multiple_of(col_ref[0] * half + i * width, width)
        copies.append(pltpu.make_async_copy(w_ref.at[:, pl.ds(first, width)], w.at[i], sems.at[i]))
        copies[-1].start()
    a = a_ref[...]
    for i, c in enumerate(copies):
        c.wait()
        cols = slice(i * width, (i + 1) * width)
        acc = dot(a, w[i])
        if last:
            acc = acc + refs[0][:, cols].astype(F32)
        out_ref[:, cols] = acc.astype(BF)


def mix_part(col, att, w, more=(), after=()):
    half = w.shape[1] // 2
    width = 512
    return call(
        functools.partial(mix_kernel, last=bool(more)), "mix_part", (S((TOK, half), BF),),
        [SM, VM, FAR] + [VM] * len(more) + [HB] * len(after),
        [pltpu.VMEM((half // width, NQ * HD, width), BF), dma(half // width)],
        (col, att, w, *more, *after), 1280, 1, 52,
    )[0]


def shift(d, swap=0):
    return [(x * 2 + c, ((x + d) % 4) * 2 + (c ^ swap)) for x in range(4) for c in range(2)]


SWAP = shift(0, 1)


def shards(
    queries, keys, values, prefix_keys, prefix_values, rollout_group, roll_length, advantage,
    upstream, w_out,
):
    ctx = lax.axis_index("ctx")
    grp = lax.axis_index("grp")
    tp = lax.axis_index("tp")
    x, core = ctx // 2, ctx % 2
    z, ylo = grp // 2, grp % 2
    xc = jnp.stack([x, core]).astype(jnp.int32)
    own_col = tp.reshape(1).astype(jnp.int32)
    other_col = 1 - own_col
    group = rollout_group[0]
    mate = lax.ppermute(rollout_group, "grp", SWAP)[0]
    positions = ctx * TOK + lax.iota(jnp.int32, TOK)
    live = (positions < roll_length[0]).astype(F32)[None]
    row = live * advantage[0]

    prefix = stack_pair(prefix_keys, prefix_values)
    spread = [prefix] + [lax.ppermute(prefix, "grp", shift(d)) for d in (1, 2, 3)]
    first = back_part(own_col, w_out, upstream[0])[0]
    qt, qn, local = turn(queries, keys, values, first)
    local_same = [lax.ppermute(local, "ctx", shift(d)) for d in (1, 2, 3)]
    local_mate, *mates = [lax.ppermute(s, "ctx", SWAP) for s in (local, *local_same)]
    pairs = [s for pair in zip(local_same, mates) for s in pair]

    places = jnp.stack([(z - mate // 2) % 4, (z - group // 2) % 4])
    sent, held = pick(places, spread, qt)
    came = lax.ppermute(sent, "grp", SWAP)
    own = jnp.where(group % 2 == ylo, held, came)
    *state, up = fwd_near(qt, local, upstream[0], own)
    up_other = lax.ppermute(up, "tp", [(0, 1), (1, 0)])
    own_mate = lax.ppermute(own, "ctx", SWAP)
    own_same = [lax.ppermute(own, "ctx", shift(d)) for d in (1, 2, 3)]
    state = fwd_far(xc, qt, state, pairs[:4], EACH[:4], 0, *pairs[4:])
    merged = merge(own_same, state[0])
    own_mates = lax.ppermute(merged, "ctx", SWAP)
    state = fwd_far(xc, qt, state, [*pairs[4:], local_mate], EACH[:3], 2, merged)
    prefix_shards = [own, own_mate, merged, own_mates]
    ot, att, lse = fwd_prefix(live, qt, state, prefix_shards)
    half = mix_part(other_col, att, w_out)
    mix_other = lax.ppermute(half, "tp", [(0, 1), (1, 0)])
    gt, gn = back_part(other_col, w_out, up_other, (first, row), (half,))
    args = (qt, qn, gt, gn, ot, lse)

    dq, same, other = bwd_prefix(args, prefix_shards)
    got = lax.ppermute(other, "ctx", SWAP)
    sums = add_pairs(same, got)
    moved = [lax.ppermute(sums[d], "ctx", shift(-d)) for d in (1, 2, 3)]
    dq, early_same, early_other = bwd_local(
        xc, args, dq, [local, local_mate, *pairs[:2]], False, sums[0], mix_other
    )
    column = add_all([sums[0]] + moved, dq)
    theirs = lax.ppermute(column, "grp", SWAP)
    grad_queries, late_same, late_other = bwd_local(xc, args, dq, pairs[2:], True, column)
    target = (z + lax.iota(jnp.int32, 4)) % 4
    flags = jnp.concatenate(
        [(g % 2 == ylo) & (g // 2 == target) for g in (group, mate)]
    ).astype(jnp.int32)
    placed = slots(flags, column, theirs, late_same)
    arrived = [lax.ppermute(placed[d], "grp", shift(d)) for d in (1, 2, 3)]
    early = add_pairs(early_same, lax.ppermute(early_other, "ctx", SWAP), placed[0])
    late = add_pairs(late_same, lax.ppermute(late_other, "ctx", SWAP), placed[0])
    sent_back = [lax.ppermute(p, "ctx", shift(-d)) for d, p in ((1, early[1]), (2, late[0]), (3, late[1]))]
    mixed = mix_part(own_col, att, w_out, (mix_other,), (late[0],))
    owned = add_all([placed[0]] + arrived)
    mine = add_all([early[0]] + sent_back)
    return (
        att[None],
        mixed[None],
        grad_queries[None],
        mine[0][None],
        mine[1][None],
        owned[0][None],
        owned[1][None],
    )


def solution(mesh):
    spec = P("grp", "ctx", "tp")
    in_specs = (spec,) * 5 + (P("grp"),) * 3 + (spec, P("tp", None))
    return jax.shard_map(
        shards, mesh=mesh, in_specs=in_specs, out_specs=(spec,) * 7, check_vma=False
    )
```
